512 devices in a mesh: ha: 16 (over y_lo, z), wa: 16 (over y_hi, x), ta: 2 (over core).
Axes of the slice: x: 4, y: 8 (y_hi: 4, y_lo: 2; y = y_hi * 2 + y_lo), z: 8, core: 2. Of those that a mesh axis runs over, the one named last changes fastest.
Arguments:
- queries: bfloat16 [128, 256, 1536], P('ha', 'wa', 'ta'), may hold values from -6 to 6
- keys_values: bfloat16 [2, 128, 256, 1536], P(None, 'ha', 'wa', 'ta'), may hold values from -6 to 6
- grad_out: bfloat16 [128, 256, 1536], P('ha', 'wa', 'ta'), may hold values from -96 to 96
- log_totals: float32 [128, 256, 12], P('ha', 'wa', 'ta'), may hold values from 6 to 8
- row_deltas: float32 [128, 256, 12], P('ha', 'wa', 'ta'), may hold values from -256 to 256
- prompt_kv: bfloat16 [2, 128, 1536], P(None, None, 'ta'), may hold values from -6 to 6
- prompt_proj: bfloat16 [2, 3072, 1536], P(None, 'ha', 'ta'), may hold values from -0.109375 to 0.109375
- neighbours: int32 [512, 9], replicated, may hold values from -1 to 511, as said below
- prompt_length: int32 [1], replicated, may hold values from 32 to 128
Outputs:
- grad_queries: bfloat16 [128, 256, 1536], P('ha', 'wa', 'ta')
- grad_keys_values: bfloat16 [2, 128, 256, 1536], P(None, 'ha', 'wa', 'ta')
- context_grad: float32 [128, 3072], P(None, 'ha')
The draws below stay inside these ranges and needn't reach their ends.
Inputs may be any that keep to these rules, and one draw needn't show every extreme that they name: `neighbours`: row t lists tile t first, then further tiles, without repeats, each within one tile of tile t in both directions, then -1 in the unused slots.
All inputs are finite; a program needn't handle non-finite values.
Results may differ from the reference program's by a relative error of at most 0.005.
Values may be sent and summed in bfloat16 or wider, within the bound.
A program may use at most 64 MiB of HBM per device.

```python
import jax
import jax.numpy as jnp
from jax import lax

TS = 8
SLOTS = 9
HEADS = 12
HEAD_DIM = 128
D = 3072
TEXT = 128
IMG_H = 128
IMG_W = 256


def draw_neighbours(key, part):
    key = jax.random.fold_in(key, 11)
    tile_rows, tile_cols = (IMG_H // TS, IMG_W // TS)
    shape_all = (tile_rows, tile_cols, SLOTS)
    tile_row = lax.broadcasted_iota(jnp.int32, shape_all, 0)
    tile_col = lax.broadcasted_iota(jnp.int32, shape_all, 1)
    slot_index = lax.broadcasted_iota(jnp.int32, shape_all, 2)
    near_row = tile_row + slot_index // 3 - 1
    near_col = tile_col + slot_index % 3 - 1
    inside = (near_row >= 0) & (near_row < tile_rows) & (near_col >= 0) & (near_col < tile_cols)
    coins = jax.random.randint(key, shape_all, 0, 4)
    centre = slot_index == 4
    keep = inside & ((coins < 3) | centre)
    numbers = jnp.where(keep, near_row * tile_cols + near_col, -1)
    ranking = jnp.where(centre, 0, jnp.where(keep, 1, 2)).astype(jnp.int32)
    order = jnp.argsort(ranking, axis=-1, stable=True)
    listed = jnp.take_along_axis(numbers, order, axis=-1)
    return listed.reshape(tile_rows * tile_cols, SLOTS).astype(jnp.int32)


def level_of(own_key, dims, cuts, least, top_value):
    level, own = 1.0, jax.random.fold_in(own_key, 6)
    for dim, blocks in cuts:
        heights = jnp.exp(jax.random.uniform(jax.random.fold_in(own, dim), (blocks,), jnp.float32, least / len(cuts), top_value / len(cuts)))
        level = level * jnp.repeat(heights, dims[dim] // blocks).reshape([-1 if axis == dim else 1 for axis in range(len(dims))])
    return level


def noise(rng, shape, scale, bound, pieces=(), kind=jnp.bfloat16):
    gain = level_of(rng, shape, pieces, -0.22, 0.18) if pieces else 1.0
    drawn = jax.random.normal(rng, shape, jnp.float32) * scale * gain
    return jnp.minimum(jnp.maximum(drawn, -bound), bound).astype(kind)


def setup_inputs(seed: int = 0) -> dict:
    key_of = jax.random.split(jax.random.key(seed), 10)
    return {
        "queries": noise(key_of[0], (IMG_H, IMG_W, HEADS * HEAD_DIM), 1.0, 6.0, ((0, 16), (1, 16), (2, 2))),
        "keys_values": noise(key_of[1], (2, IMG_H, IMG_W, HEADS * HEAD_DIM), 1.0, 6.0, ((1, 16), (2, 16), (3, 2))),
        "grad_out": noise(key_of[2], (IMG_H, IMG_W, HEADS * HEAD_DIM), 16.0, 96.0, ((0, 16), (1, 16), (2, 2))),
        "log_totals": jnp.clip(6.0 + 2.0 * jax.random.uniform(key_of[3], (IMG_H, IMG_W, HEADS), jnp.float32) ** level_of(key_of[3], (IMG_H, IMG_W, HEADS), ((0, 16), (1, 16), (2, 2)), -0.2, 0.2), 6.0, 8.0),
        "row_deltas": noise(key_of[4], (IMG_H, IMG_W, HEADS), 40.0, 256.0, ((0, 16), (1, 16), (2, 2)), jnp.float32),
        "prompt_kv": noise(key_of[5], (2, TEXT, HEADS * HEAD_DIM), 1.0, 6.0, ((2, 2),)),
        "prompt_proj": noise(key_of[6], (2, D, HEADS * HEAD_DIM), D ** -0.5, 0.109375, ((1, 16), (2, 2))),
        "neighbours": draw_neighbours(jax.random.fold_in(key_of[9], 71), 0),
        "prompt_length": jax.random.randint(key_of[8], (1,), TEXT // 4, TEXT + 1).astype(jnp.int32),
    }


NEIGHBOUR_STEPS = [(row_step, col_step) for row_step in (-1, 0, 1) for col_step in (-1, 0, 1)]


def tile_grid(values_field, tile_side):
    height, breadth = values_field.shape[0], values_field.shape[1]
    remains = values_field.shape[2:]
    blocks = values_field.reshape((height // tile_side, tile_side, breadth // tile_side, tile_side) + remains)
    blocks = jnp.swapaxes(blocks, 1, 2)
    return blocks.reshape((height // tile_side, breadth // tile_side, tile_side * tile_side) + remains)


def untile(tile_field, tile_side):
    remains = tile_field.shape[3:]
    blocks = tile_field.reshape(tile_field.shape[:2] + (tile_side, tile_side) + remains)
    blocks = jnp.swapaxes(blocks, 1, 2)
    return blocks.reshape((tile_field.shape[0] * tile_side, tile_field.shape[1] * tile_side) + remains)


def rounded(values):
    return lax.optimization_barrier(values.astype(jnp.bfloat16)).astype(jnp.float32)


def block_grads(queries, out_grads, log_total, row_delta, key_rows, value_rows, allowed):
    factor = queries.shape[-1] ** -0.5
    highest = lax.Precision.HIGHEST
    scores = jnp.einsum("nmhe,nkhe->nhmk", queries, key_rows, precision=highest) * factor
    shifted = scores - jnp.swapaxes(log_total, 1, 2)[..., None]
    probability = jnp.where(allowed[:, None, None, :], jnp.exp(shifted), 0.0)
    prob_grads = jnp.einsum("nmhe,nkhe->nhmk", out_grads, value_rows, precision=highest)
    score_grads = rounded(factor * probability * (prob_grads - jnp.swapaxes(row_delta, 1, 2)[..., None]))
    grad_q = jnp.einsum("nhmk,nkhe->nmhe", score_grads, key_rows, precision=highest)
    grad_k = jnp.einsum("nhmk,nmhe->nkhe", score_grads, queries, precision=highest)
    grad_v = jnp.einsum("nhmk,nmhe->nkhe", rounded(probability), out_grads, precision=highest)
    return grad_q, grad_k, grad_v


def allowed_tiles(neighbours, tile_rows, tile_cols):
    numbers = jnp.arange(tile_rows * tile_cols, dtype=jnp.int32).reshape(tile_rows, tile_cols)
    padded = jnp.pad(numbers, 1, constant_values=-2)
    listed = neighbours.reshape(tile_rows, tile_cols, neighbours.shape[-1])
    mask_list = []
    for row_step, col_step in NEIGHBOUR_STEPS:
        target = padded[1 + row_step:1 + row_step + tile_rows, 1 + col_step:1 + col_step + tile_cols]
        mask_list.append(jnp.any(listed == target[:, :, None], axis=-1))
    return jnp.stack(mask_list, axis=-1)


def pad_tiles(values_field):
    return jnp.pad(values_field, ((1, 1), (1, 1)) + ((0, 0),) * (values_field.ndim - 2))


def reference(queries, keys_values, grad_out, log_totals, row_deltas, prompt_kv, prompt_proj, neighbours, prompt_length):
    tile_rows, tile_cols = IMG_H // TS, IMG_W // TS
    cells = TS * TS
    width = HEADS * HEAD_DIM

    def split_heads(values_field):
        return values_field.reshape(values_field.shape[:-1] + (HEADS, HEAD_DIM)).astype(jnp.float32)

    query_pad = pad_tiles(tile_grid(split_heads(queries), TS))
    gradout_pad = pad_tiles(tile_grid(split_heads(grad_out), TS))
    key_pad = pad_tiles(tile_grid(split_heads(keys_values[0]), TS))
    value_pad = pad_tiles(tile_grid(split_heads(keys_values[1]), TS))
    total_pad = pad_tiles(tile_grid(log_totals, TS))
    delta_pad = pad_tiles(tile_grid(row_deltas, TS))
    allowed_pad = pad_tiles(allowed_tiles(neighbours, tile_rows, tile_cols))
    prompt_keys = split_heads(prompt_kv[0])[None]
    prompt_values = split_heads(prompt_kv[1])[None]
    prompt_live = (jnp.arange(TEXT, dtype=jnp.int32) < prompt_length[0])[None, :]

    def pick(values_field, row_index, col_start):
        return lax.dynamic_index_in_dim(values_field, row_index, 0, keepdims=False)[col_start:col_start + tile_cols]

    def one_row(carry, row_index):
        own_q = pick(query_pad, row_index + 1, 1)
        own_g = pick(gradout_pad, row_index + 1, 1)
        own_t = pick(total_pad, row_index + 1, 1)
        own_d = pick(delta_pad, row_index + 1, 1)
        own_k = pick(key_pad, row_index + 1, 1)
        own_v = pick(value_pad, row_index + 1, 1)
        own_a = pick(allowed_pad, row_index + 1, 1)
        grad_query = jnp.zeros(own_q.shape, jnp.float32)
        grad_key = jnp.zeros(own_k.shape, jnp.float32)
        grad_value = jnp.zeros(own_v.shape, jnp.float32)
        for step_index, (row_step, col_step) in enumerate(NEIGHBOUR_STEPS):
            near_keys = pick(key_pad, row_index + 1 + row_step, 1 + col_step)
            near_values = pick(value_pad, row_index + 1 + row_step, 1 + col_step)
            near_mask = jnp.broadcast_to(own_a[:, step_index][:, None], (tile_cols, cells))
            grad_query = grad_query + block_grads(own_q, own_g, own_t, own_d, near_keys, near_values, near_mask)[0]
            back_row, back_col = row_index + 1 - row_step, 1 - col_step
            far_mask = jnp.broadcast_to(pick(allowed_pad, back_row, back_col)[:, step_index][:, None], (tile_cols, cells))
            far_parts = block_grads(pick(query_pad, back_row, back_col), pick(gradout_pad, back_row, back_col),
                                    pick(total_pad, back_row, back_col), pick(delta_pad, back_row, back_col),
                                    own_k, own_v, far_mask)
            grad_key = grad_key + far_parts[1]
            grad_value = grad_value + far_parts[2]
        flat_rows = (1, tile_cols * cells, HEADS, HEAD_DIM)
        prompt_parts = block_grads(own_q.reshape(flat_rows), own_g.reshape(flat_rows),
                                   own_t.reshape(1, tile_cols * cells, HEADS), own_d.reshape(1, tile_cols * cells, HEADS),
                                   prompt_keys, prompt_values, prompt_live)
        grad_query = grad_query + prompt_parts[0].reshape(own_q.shape)
        carry = (carry[0] + prompt_parts[1][0], carry[1] + prompt_parts[2][0])
        return carry, (grad_query, grad_key, grad_value)

    start = (jnp.zeros((TEXT, HEADS, HEAD_DIM), jnp.float32), jnp.zeros((TEXT, HEADS, HEAD_DIM), jnp.float32))
    sums, row_outs = lax.scan(one_row, start, jnp.arange(tile_rows, dtype=jnp.int32))

    def to_field(tile_field):
        return untile(tile_field, TS).reshape(IMG_H, IMG_W, width).astype(jnp.bfloat16)

    grad_queries = to_field(row_outs[0])
    grad_keys_values = jnp.stack([to_field(row_outs[1]), to_field(row_outs[2])])
    prompt_grads = jnp.stack([sums[0], sums[1]]).reshape(2, TEXT, width).astype(jnp.bfloat16)
    context_grad = jnp.dot(prompt_grads[0], prompt_proj[0].T, preferred_element_type=jnp.float32)
    context_grad = context_grad + jnp.dot(prompt_grads[1], prompt_proj[1].T, preferred_element_type=jnp.float32)
    return grad_queries, grad_keys_values, context_grad
```

```python
import functools

import jax
import jax.numpy as jnp
from jax import lax
from jax.experimental import pallas as pl
from jax.experimental.pallas import tpu as pltpu
from jax.sharding import PartitionSpec as P

MESH = pl.DeviceIdType.MESH
F32 = jnp.float32
BF16 = jnp.bfloat16
TS = 8
CELLS = TS * TS
HD = 128
BIG = 1e30
STEPS = [(-1, 0), (1, 0), (0, -1), (0, 1), (-1, -1), (-1, 1), (1, -1), (1, 1)]


def block_of(row_step, col_step):
    return row_step + 1 if col_step == 0 else row_step + 4


def rows_of(col_step):
    return {0: slice(0, 128), -1: slice(0, 64), 1: slice(64, 128)}[col_step]


def nt(a, b):
    return lax.dot_general(a, b, (((1,), (1,)), ((), ())), preferred_element_type=F32)


def nn(a, b):
    return lax.dot_general(a, b, (((1,), (0,)), ((), ())), preferred_element_type=F32)


def tn(a, b):
    return lax.dot_general(a, b, (((0,), (0,)), ((), ())), preferred_element_type=F32)


def kernel(
    nh, nw, heads, per_owner,
    q_hbm, kv_hbm, g_hbm, lt_hbm, rd_hbm, pkv_hbm, proj_hbm, nb_hbm, plen_ref,
    dq_out, dkv_out, ctx_out,
    qn, kv, gn, ltn, rdn, pkv, proj, nb,
    qg, lrx, lro, pen, picked, dq_acc, dq_send, dq_recv, dkv_acc,
    ps, pr, t2, r2, s2, g2, c3, c4,
    ld_sem, qg_ss, qg_rs, lr_ss, lr_rs, dq_ss, dq_rs,
    p1_ss, p1_rs, p2_ss, p2_rs, p3_ss, p3_rs, c3_ss, c3_rs, c4_ss, c4_rs,
):
    width = heads * HD
    ia, iw, it = lax.axis_index("ha"), lax.axis_index("wa"), lax.axis_index("ta")
    factor = HD ** -0.5
    tr = 128 // nw

    def at(row_step, col_step):
        return (lax.rem(ia + row_step + nh, nh), lax.rem(iw + col_step + nw, nw), it)

    barrier = pltpu.get_barrier_semaphore()

    def greet(who):
        pl.semaphore_signal(barrier, inc=1, device_id=who, device_id_type=MESH)

    def greet_wa(i, c):
        greet((ia, lax.rem(iw + i, nw), it))
        return c

    def greet_ha(i, c):
        greet((lax.rem(ia + i, nh), iw, it))
        return c

    for step in STEPS[4:]:
        greet(at(*step))
    lax.fori_loop(1, nw, greet_wa, 0)
    lax.fori_loop(1, nh, greet_ha, 0)
    greet((ia, iw, 1 - it))

    loads = [
        pltpu.make_async_copy(src, dst, ld_sem.at[n])
        for n, (src, dst) in enumerate(
            [(q_hbm, qn), (g_hbm, gn), (lt_hbm, ltn), (rd_hbm, rdn), (nb_hbm, nb),
             (pkv_hbm, pkv), (kv_hbm, kv), (proj_hbm, proj)]
        )
    ]
    for load in loads:
        load.start()

    for n, source in ((0, qn), (1, gn)):
        loads[n].wait()
        for i in range(4):
            x = source[32 * i:32 * i + 32, :].astype(F32)
            qg[1, n, 16 * i:16 * i + 16, :] = jnp.concatenate([x[0:8], x[16:24]], 0).astype(BF16)
            qg[1, n, 64 + 16 * i:80 + 16 * i, :] = jnp.concatenate([x[8:16], x[24:32]], 0).astype(BF16)
    for n, source in ((0, ltn), (1, rdn)):
        loads[2 + n].wait()
        x = source[...].reshape(TS, 2, TS, heads)
        x = jnp.concatenate([x[:, 0].reshape(CELLS, heads), x[:, 1].reshape(CELLS, heads)], 0)
        x = jnp.concatenate([x, jnp.zeros((128, 128 - heads), F32)], 1)
        lro[1, 8 * n:8 * n + 8, :] = x.T[0:8]

    pl.semaphore_wait(barrier, 4 + (nw - 1) + (nh - 1) + 1)

    def qg_copy(n):
        dr, dc = STEPS[n]
        return pltpu.make_async_remote_copy(
            src_ref=qg.at[1, :, rows_of(-dc), :],
            dst_ref=qg.at[block_of(dr, dc), :, rows_of(dc), :],
            send_sem=qg_ss.at[n], recv_sem=qg_rs.at[n],
            device_id=at(-dr, -dc), device_id_type=MESH,
        )

    def lr_copy(n):
        dr, dc = STEPS[n]
        return pltpu.make_async_remote_copy(
            src_ref=lro.at[1], dst_ref=lrx.at[n],
            send_sem=lr_ss.at[n], recv_sem=lr_rs.at[n],
            device_id=at(-dr, -dc), device_id_type=MESH,
        )

    def dq_copy(n):
        dr, dc = STEPS[n]
        return pltpu.make_async_remote_copy(
            src_ref=dq_send.at[block_of(dr, dc), rows_of(dc), :],
            dst_ref=dq_recv.at[block_of(-dr, -dc), rows_of(-dc), :],
            send_sem=dq_ss.at[n], recv_sem=dq_rs.at[n],
            device_id=at(dr, dc), device_id_type=MESH,
        )

    for n in range(8):
        lr_copy(n).start()
    for n in range(8):
        qg_copy(n).start()

    loads[5].wait()
    live = lax.broadcasted_iota(jnp.int32, (128, 128), 0) < plen_ref[0]
    for h in range(heads):
        hs = slice(HD * h, HD * h + HD)
        k, v, q, g = pkv[0, :, hs], pkv[1, :, hs], qg[1, 0, :, hs], qg[1, 1, :, hs]
        p = jnp.exp(jnp.where(live, nt(k, q) * factor - lro[1, h:h + 1, :], -BIG))
        ds = (factor * p * (nt(v, g) - lro[1, 8 + h:9 + h, :])).astype(BF16)
        dk = nn(ds, q).reshape(nw, tr, HD)
        dv = nn(p.astype(BF16), g).reshape(nw, tr, HD)
        ps[:, :, hs] = jnp.concatenate([dk, dv], 1).astype(BF16)
        dq_acc[:, hs] = tn(ds, k)

    def p1_copy(peer, slot):
        return pltpu.make_async_remote_copy(
            src_ref=ps.at[peer], dst_ref=pr.at[slot], send_sem=p1_ss.at[peer],
            recv_sem=p1_rs.at[slot], device_id=(ia, peer, it), device_id_type=MESH,
        )

    def p2_copy(peer, slot):
        return pltpu.make_async_remote_copy(
            src_ref=t2.at[peer], dst_ref=r2.at[slot], send_sem=p2_ss.at[peer],
            recv_sem=p2_rs.at[slot], device_id=(peer, iw, it), device_id_type=MESH,
        )

    def p3_copy(peer, slot):
        return pltpu.make_async_remote_copy(
            src_ref=s2, dst_ref=g2.at[slot], send_sem=p3_ss.at[peer],
            recv_sem=p3_rs.at[slot], device_id=(peer, iw, it), device_id_type=MESH,
        )

    def c4_copy(peer, slot):
        return pltpu.make_async_remote_copy(
            src_ref=c4.at[iw], dst_ref=c4.at[slot], send_sem=c4_ss.at[peer],
            recv_sem=c4_rs.at[slot], device_id=(ia, peer, it), device_id_type=MESH,
        )

    def start_all(copy, me, count):
        def body(i, c):
            copy(lax.rem(me + i, count), me).start()
            return c
        lax.fori_loop(1, count, body, 0)

    def wait_all(copy, me, count):
        def body(i, c):
            other = lax.rem(me + i, count)
            copy(other, other).wait_recv()
            return c
        lax.fori_loop(1, count, body, 0)

    def wait_sent(copy, me, count):
        def body(i, c):
            copy(lax.rem(me + i, count), me).wait_send()
            return c
        lax.fori_loop(1, count, body, 0)

    start_all(p1_copy, iw, nw)

    loads[4].wait()
    cols = 2 * nw
    lane = lax.broadcasted_iota(jnp.int32, (1, 128), 1)
    tiles = [(r - 1, c) for r in range(3) for c in (0, 1)] + [(r - 1, c) for r in range(3) for c in (-1, 2)]
    for n, (r, c) in enumerate(tiles):
        row, col = ia + r, 2 * iw + c
        fine = (row >= 0) & (row < nh) & (col >= 0) & (col < cols)
        number = jnp.where(fine, row * cols + col, 0)
        picked[n:n + 1, :] = jnp.where(fine, nb[pl.ds(number, 1), :], -1)
    listed = picked[0:12, :]
    own = ia * cols + 2 * iw
    for side in range(2):
        hit = jnp.max(jnp.where(listed == own + side, 1.0, 0.0), axis=1, keepdims=True)
        hit = jnp.broadcast_to(hit, (12, 128))
        for b in range(6):
            pen[b, side:side + 1, :] = BIG * (1.0 - jnp.where(lane < 64, hit[2 * b:2 * b + 1], hit[2 * b + 1:2 * b + 2]))

    loads[6].wait()

    def attend(b, first=False):
        for h in range(heads):
            hs = slice(HD * h, HD * h + HD)
            k, v, q, g = kv[0, :, hs], kv[1, :, hs], qg[b, 0, :, hs], qg[b, 1, :, hs]
            total = (lro[b, h:h + 1, :] + pen[b, 0:2, :]).reshape(1, 2, 1, 128)
            p = jnp.exp(nt(k, q).reshape(TS, 2, TS, 128) * factor - total).reshape(128, 128)
            ds = (factor * p * (nt(v, g) - lro[b, 8 + h:9 + h, :])).astype(BF16)
            dk, dv = nn(ds, q), nn(p.astype(BF16), g)
            if first:
                dkv_acc[0, :, hs] = dk
                dkv_acc[1, :, hs] = dv
                dq_acc[:, hs] += tn(ds, k)
            else:
                dkv_acc[0, :, hs] += dk
                dkv_acc[1, :, hs] += dv
                dq_send[b, :, hs] = tn(ds, k).astype(BF16)

    def attend_centre(n):
        b = block_of(*STEPS[n])
        lr_copy(n).wait_recv()
        lro[b] = lrx[n]
        qg_copy(n).wait_recv()
        attend(b)
        dq_copy(n).start()

    def attend_outer(west, east):
        b = block_of(*STEPS[west])
        lr_copy(west).wait_recv()
        lr_copy(east).wait_recv()
        both = jnp.where(lax.broadcasted_iota(jnp.int32, (16, 128), 1) < 64, lrx[east], lrx[west])
        lro[b] = pltpu.roll(both, 64, 1)
        qg_copy(west).wait_recv()
        qg_copy(east).wait_recv()
        attend(b)
        dq_copy(west).start()
        dq_copy(east).start()

    attend(1, first=True)
    attend_outer(2, 3)

    wait_all(p1_copy, iw, nw)
    pr[iw] = ps[iw]
    acc = jnp.zeros((2 * tr, width), F32)
    for j in range(nw):
        acc = acc + pr[j].astype(F32)
    t2[...] = jnp.zeros_like(t2)
    for j in range(2 * tr // 8):
        for h in range(heads):
            n = j * heads + h
            t2[n // per_owner, n % per_owner] = acc[8 * j:8 * j + 8, HD * h:HD * h + HD]
    start_all(p2_copy, ia, nh)

    attend_centre(0)
    attend_centre(1)

    wait_all(p2_copy, ia, nh)
    r2[ia] = t2[ia]
    acc = r2[0]
    for j in range(1, nh):
        acc = acc + r2[j]
    s2[...] = acc
    start_all(p3_copy, ia, nh)

    attend_outer(4, 5)

    wait_all(p3_copy, ia, nh)
    g2[ia] = s2[...]
    loads[7].wait()
    groups = []
    for j in range(2 * tr // 8):
        tiles = [g2[(j * heads + h) // per_owner, (j * heads + h) % per_owner] for h in range(heads)]
        groups.append(jnp.concatenate(tiles, 1))
    half = len(groups) // 2
    part = nt(jnp.concatenate(groups[:half], 0).astype(BF16), proj[0])
    part = part + nt(jnp.concatenate(groups[half:], 0).astype(BF16), proj[1])
    c3[0] = part
    c3_copy = pltpu.make_async_remote_copy(
        src_ref=c3.at[0], dst_ref=c3.at[1], send_sem=c3_ss, recv_sem=c3_rs,
        device_id=(ia, iw, 1 - it), device_id_type=MESH,
    )
    c3_copy.start()

    attend_outer(6, 7)
    for n in range(2):
        for i in range(4):
            dkv_out[n, 32 * i:32 * i + 32, :] = dkv_acc[n, 32 * i:32 * i + 32, :].astype(BF16)

    c3_copy.wait_recv()
    c4[iw] = c3[0] + c3[1]
    start_all(c4_copy, iw, nw)

    for n in range(8):
        dq_copy(n).wait_recv()
    for i in range(4):
        left, right = slice(16 * i, 16 * i + 16), slice(64 + 16 * i, 80 + 16 * i)
        sums = []
        for rows in (left, right):
            x = dq_acc[rows, :]
            for b in (0, 2, 3, 4, 5):
                x = x + dq_recv[b, rows, :].astype(F32)
            sums.append(x)
        a, b = sums
        dq_out[32 * i:32 * i + 32, :] = jnp.concatenate([a[0:8], b[0:8], a[8:16], b[8:16]], 0).astype(BF16)

    wait_all(c4_copy, iw, nw)
    for j in range(nw):
        ctx_out[tr * j:tr * j + tr, :] = c4[j]

    for n in range(8):
        qg_copy(n).wait_send()
        lr_copy(n).wait_send()
        dq_copy(n).wait_send()
    c3_copy.wait_send()
    wait_sent(p1_copy, iw, nw)
    wait_sent(p2_copy, ia, nh)
    wait_sent(p3_copy, ia, nh)
    wait_sent(c4_copy, iw, nw)


def solution(mesh):
    nh, nw = mesh.shape["ha"], mesh.shape["wa"]

    def local(queries, keys_values, grad_out, log_totals, row_deltas, prompt_kv, prompt_proj, neighbours, prompt_length):
        rows_here, cols_here, width = queries.shape
        heads = log_totals.shape[-1]
        cells = rows_here * cols_here
        text = prompt_kv.shape[1]
        outs = prompt_proj.shape[1]
        tr = text // nw
        count = 2 * tr // 8 * heads
        per_owner = -(-count // nh)
        any_space = pl.BlockSpec(memory_space=pl.ANY)
        vmem = pl.BlockSpec(memory_space=pltpu.VMEM)
        dma = pltpu.SemaphoreType.DMA
        listed = jnp.pad(neighbours, ((0, 0), (0, 128 - neighbours.shape[1])), constant_values=-1)
        dq, dkv, ctx = pl.pallas_call(
            functools.partial(kernel, nh, nw, heads, per_owner),
            out_shape=(
                jax.ShapeDtypeStruct((cells, width), BF16),
                jax.ShapeDtypeStruct((2, cells, width), BF16),
                jax.ShapeDtypeStruct((text, outs), F32),
            ),
            in_specs=[any_space] * 8 + [pl.BlockSpec(memory_space=pltpu.SMEM)],
            out_specs=(vmem, vmem, vmem),
            scratch_shapes=[
                pltpu.VMEM((cells, width), BF16),
                pltpu.VMEM((2, cells, width), BF16),
                pltpu.VMEM((cells, width), BF16),
                pltpu.VMEM((cells, heads), F32),
                pltpu.VMEM((cells, heads), F32),
                pltpu.VMEM((2, text, width), BF16),
                pltpu.VMEM((2, outs, width), BF16),
                pltpu.VMEM((neighbours.shape[0], 128), jnp.int32),
                pltpu.VMEM((6, 2, cells, width), BF16),
                pltpu.VMEM((8, 16, cells), F32),
                pltpu.VMEM((6, 16, cells), F32),
                pltpu.VMEM((6, 8, cells), F32),
                pltpu.VMEM((16, 128), jnp.int32),
                pltpu.VMEM((cells, width), F32),
                pltpu.VMEM((6, cells, width), BF16),
                pltpu.VMEM((6, cells, width), BF16),
                pltpu.VMEM((2, cells, width), F32),
                pltpu.VMEM((nw, 2 * tr, width), BF16),
                pltpu.VMEM((nw, 2 * tr, width), BF16),
                pltpu.VMEM((nh, per_owner, 8, HD), F32),
                pltpu.VMEM((nh, per_owner, 8, HD), F32),
                pltpu.VMEM((per_owner, 8, HD), F32),
                pltpu.VMEM((nh, per_owner, 8, HD), F32),
                pltpu.VMEM((2, tr, outs), F32),
                pltpu.VMEM((nw, tr, outs), F32),
                dma((8,)),
                dma((8,)), dma((8,)), dma((8,)), dma((8,)), dma((8,)), dma((8,)),
                dma((nw,)), dma((nw,)), dma((nh,)), dma((nh,)), dma((nh,)), dma((nh,)),
                dma, dma, dma((nw,)), dma((nw,)),
            ],
            compiler_params=pltpu.CompilerParams(
                collective_id=0, has_side_effects=True, vmem_limit_bytes=48 * 2**20
            ),
            name="tile_attention_grads",
        )(
            queries.reshape(cells, width), keys_values.reshape(2, cells, width), grad_out.reshape(cells, width),
            log_totals.reshape(cells, heads), row_deltas.reshape(cells, heads),
            prompt_kv, prompt_proj, listed, prompt_length,
        )
        return (
            dq.reshape(rows_here, cols_here, width),
            dkv.reshape(2, rows_here, cols_here, width),
            ctx,
        )

    placed = P("ha", "wa", "ta")
    return jax.shard_map(
        local,
        mesh=mesh,
        in_specs=(placed, P(None, "ha", "wa", "ta"), placed, placed, placed, P(None, None, "ta"), P(None, "ha", "ta"), P(), P()),
        out_specs=(placed, P(None, "ha", "wa", "ta"), P(None, "ha")),
        check_vma=False,
    )
```

```python
import functools

import jax
import jax.numpy as jnp
from jax import lax
from jax.experimental import pallas as pl
from jax.experimental.pallas import tpu as pltpu
from jax.sharding import PartitionSpec as P

MESH = pl.DeviceIdType.MESH
F32 = jnp.float32
BF16 = jnp.bfloat16
TS = 8
CELLS = TS * TS
HD = 128
BIG = 1e30
RING_X = 4
RING_Z = 8
CHUNKS = 2
STEPS = [(-1, 0), (1, 0), (0, -1), (0, 1), (-1, -1), (-1, 1), (1, -1), (1, 1)]
SIDES = (-1, 1)


def block_of(row_step, col_step):
    return row_step + 1 if col_step == 0 else row_step + 4


def rows_of(col_step):
    return {0: slice(0, 128), -1: slice(0, 64), 1: slice(64, 128)}[col_step]


def bit(step):
    return (step + 1) // 2


def nt(a, b):
    return lax.dot_general(a, b, (((1,), (1,)), ((), ())), preferred_element_type=F32)


def nn(a, b):
    return lax.dot_general(a, b, (((1,), (0,)), ((), ())), preferred_element_type=F32)


def tn(a, b):
    return lax.dot_general(a, b, (((0,), (0,)), ((), ())), preferred_element_type=F32)


def kernel(
    nh, nw, heads, per_owner,
    q_hbm, kv_hbm, g_hbm, lt_hbm, rd_hbm, pkv_hbm, proj_hbm, nb_hbm, plen_ref,
    dq_out, dkv_out, ctx_out,
    qn, kv, gn, ltn, rdn, pkv, proj, nb,
    qg, lrx, lro, pen, dqf, dq_send, dq_recv, cx, cz, dkv_acc,
    ps, pa, s1, pb, t2, r2, s2, g2, c3, c4,
    ld_sem, qg_ss, qg_rs, fw_ss, lr_ss, lr_rs, dq_ss, dq_rs, co_ss, cx_rs, cz_rs,
    pa_ss, pa_rs, pb_ss, pb_rs, p2_ss, p2_rs, p3_ss, p3_rs, c3_ss, c3_rs, cy_ss, cy_rs, cw_ss, cw_rs,
):
    width = heads * HD
    nx = min(RING_X, nw)
    ny = nw // nx
    ia, iw, it = lax.axis_index("ha"), lax.axis_index("wa"), lax.axis_index("ta")
    ix, iy = lax.rem(iw, nx), iw // nx
    factor = HD ** -0.5
    tr = 128 // nw
    per_chunk = heads // CHUNKS

    def place(row_step, col_step):
        return lax.rem(ia + row_step + nh, nh), lax.rem(iw + col_step + nw, nw)

    def at(row_step, col_step):
        return place(row_step, col_step) + (it,)

    def seam(column, side):
        return lax.rem(column, RING_X) == (0 if side < 0 else RING_X - 1)

    def by_x(who, row_step, side):
        row, column = who
        across = lax.rem(row, RING_Z) == (0 if row_step < 0 else RING_Z - 1)
        return jnp.logical_or(jnp.logical_not(seam(column, side)), across)

    def lanes(c):
        return slice(HD * per_chunk * c, HD * per_chunk * (c + 1))

    barrier = pltpu.get_barrier_semaphore()

    def greet(who):
        pl.semaphore_signal(barrier, inc=1, device_id=who, device_id_type=MESH)

    def x_peer(i):
        return iy * nx + lax.rem(ix + i, nx)

    def y_peer(i):
        return lax.rem(iy + i, ny) * nx + ix

    def h_peer(i):
        return lax.rem(ia + i, nh)

    def greet_ha(i, c):
        greet((h_peer(i), iw, it))
        return c

    for step in STEPS:
        greet(at(*step))
    for i in range(1, nx):
        greet((ia, x_peer(i), it))
    for i in range(1, ny):
        greet((ia, y_peer(i), it))
    lax.fori_loop(1, nh, greet_ha, 0)
    greet((ia, iw, 1 - it))

    loads = [
        pltpu.make_async_copy(src, dst, ld_sem.at[n])
        for n, (src, dst) in enumerate(
            [(q_hbm, qn), (g_hbm, gn), (lt_hbm, ltn), (rd_hbm, rdn), (nb_hbm, nb),
             (pkv_hbm, pkv), (kv_hbm, kv), (proj_hbm, proj)]
        )
    ]
    for load in loads:
        load.start()

    for n, source in ((0, qn), (1, gn)):
        loads[n].wait()
        for i in range(4):
            x = source[32 * i:32 * i + 32, :].astype(F32)
            qg[1, n, 16 * i:16 * i + 16, :] = jnp.concatenate([x[0:8], x[16:24]], 0).astype(BF16)
            qg[1, n, 64 + 16 * i:80 + 16 * i, :] = jnp.concatenate([x[8:16], x[24:32]], 0).astype(BF16)
    for n, source in ((0, ltn), (1, rdn)):
        loads[2 + n].wait()
        pieces = [source[:, r, TS * s:TS * s + TS] for s in (0, 1) for r in range(TS)]
        lro[1, 8 * n:8 * n + heads, :] = jnp.concatenate(pieces, 1)

    pl.semaphore_wait(barrier, 8 + (nx - 1) + (ny - 1) + (nh - 1) + 1)

    def qg_copy(n, c):
        dr, dc = STEPS[n]
        return pltpu.make_async_remote_copy(
            src_ref=qg.at[1, :, rows_of(-dc), lanes(c)],
            dst_ref=qg.at[block_of(dr, dc), :, rows_of(dc), lanes(c)],
            send_sem=qg_ss.at[c, n % 4], recv_sem=qg_rs.at[c, n],
            device_id=at(-dr, -dc), device_id_type=MESH,
        )

    def forward_x(dr, t, c):
        return pltpu.make_async_remote_copy(
            src_ref=qg.at[block_of(dr, 0), :, rows_of(t), lanes(c)],
            dst_ref=qg.at[block_of(dr, -t), :, rows_of(-t), lanes(c)],
            send_sem=fw_ss.at[c, 2 * bit(dr) + bit(t)], recv_sem=qg_rs.at[c, STEPS.index((dr, -t))],
            device_id=at(0, t), device_id_type=MESH,
        )

    def forward_z(e, s, c):
        return pltpu.make_async_remote_copy(
            src_ref=qg.at[block_of(0, s), :, rows_of(s), lanes(c)],
            dst_ref=qg.at[block_of(-e, s), :, rows_of(s), lanes(c)],
            send_sem=fw_ss.at[c, 4 + 2 * bit(e) + bit(s)], recv_sem=qg_rs.at[c, STEPS.index((-e, s))],
            device_id=at(e, 0), device_id_type=MESH,
        )

    def lr_copy(n):
        dr, dc = STEPS[n]
        return pltpu.make_async_remote_copy(
            src_ref=lro.at[1], dst_ref=lrx.at[n],
            send_sem=lr_ss.at[n], recv_sem=lr_rs.at[n],
            device_id=at(-dr, -dc), device_id_type=MESH,
        )

    def dq_copy(n, c):
        dr, dc = STEPS[n]
        return pltpu.make_async_remote_copy(
            src_ref=dq_send.at[block_of(dr, dc), rows_of(dc), lanes(c)],
            dst_ref=dq_recv.at[block_of(-dr, -dc), rows_of(-dc), lanes(c)],
            send_sem=dq_ss.at[c, n], recv_sem=dq_rs.at[c, n],
            device_id=at(dr, dc), device_id_type=MESH,
        )

    def corner_x(dr, s, c):
        return pltpu.make_async_remote_copy(
            src_ref=dq_send.at[block_of(dr, s), rows_of(s), lanes(c)],
            dst_ref=cx.at[bit(dr), bit(-s), :, lanes(c)],
            send_sem=co_ss.at[c, 2 * bit(dr) + bit(s)], recv_sem=cx_rs.at[c, 2 * bit(dr) + bit(-s)],
            device_id=at(0, s), device_id_type=MESH,
        )

    def corner_z(dr, s, c):
        return pltpu.make_async_remote_copy(
            src_ref=dq_send.at[block_of(dr, s), rows_of(s), lanes(c)],
            dst_ref=cz.at[bit(-dr), bit(s), :, lanes(c)],
            send_sem=co_ss.at[c, 2 * bit(dr) + bit(s)], recv_sem=cz_rs.at[c, 2 * bit(-dr) + bit(s)],
            device_id=at(dr, 0), device_id_type=MESH,
        )

    mine = {(dr, s): by_x((ia, iw), dr, s) for dr in SIDES for s in SIDES}
    relay_x = {(dr, t): by_x(place(0, t), dr, -t) for dr in SIDES for t in SIDES}
    relay_z = {(e, s): jnp.logical_not(by_x(place(e, 0), -e, s)) for e in SIDES for s in SIDES}
    at_seam = {s: seam(iw, s) for s in SIDES}

    for c in range(CHUNKS):
        for n in (2, 3, 0, 1):
            qg_copy(n, c).start()
    for n in range(8):
        lr_copy(n).start()

    loads[5].wait()
    live = lax.broadcasted_iota(jnp.int32, (128, 128), 0) < plen_ref[0]
    for h in range(heads):
        hs = slice(HD * h, HD * h + HD)
        k, v, q, g = pkv[0, :, hs], pkv[1, :, hs], qg[1, 0, :, hs], qg[1, 1, :, hs]
        p = jnp.exp(jnp.where(live, nt(k, q) * factor - lro[1, h:h + 1, :], -BIG))
        ds = (factor * p * (nt(v, g) - lro[1, 8 + h:9 + h, :])).astype(BF16)
        dk = nn(ds, q).reshape(nw, tr, HD)
        dv = nn(p.astype(BF16), g).reshape(nw, tr, HD)
        ps[:, :, hs] = jnp.concatenate([dk, dv], 1).astype(BF16)
        dqf[1, :, hs] = tn(ds, k)

    def pa_copy(i):
        return pltpu.make_async_remote_copy(
            src_ref=ps.at[pl.ds(lax.rem(ix + i, nx) * ny, ny)], dst_ref=pa.at[ix],
            send_sem=pa_ss.at[i], recv_sem=pa_rs.at[i], device_id=(ia, x_peer(i), it), device_id_type=MESH,
        )

    def pb_copy(i):
        return pltpu.make_async_remote_copy(
            src_ref=s1.at[lax.rem(iy + i, ny)], dst_ref=pb.at[iy],
            send_sem=pb_ss.at[i], recv_sem=pb_rs.at[i], device_id=(ia, y_peer(i), it), device_id_type=MESH,
        )

    def p2_copy(peer, slot):
        return pltpu.make_async_remote_copy(
            src_ref=t2.at[peer], dst_ref=r2.at[slot], send_sem=p2_ss.at[peer],
            recv_sem=p2_rs.at[slot], device_id=(peer, iw, it), device_id_type=MESH,
        )

    def p3_copy(peer, slot):
        return pltpu.make_async_remote_copy(
            src_ref=s2, dst_ref=g2.at[slot], send_sem=p3_ss.at[peer],
            recv_sem=p3_rs.at[slot], device_id=(peer, iw, it), device_id_type=MESH,
        )

    def cy_copy(i):
        own_slot = ix * ny + iy
        return pltpu.make_async_remote_copy(
            src_ref=c4.at[own_slot], dst_ref=c4.at[own_slot],
            send_sem=cy_ss.at[i], recv_sem=cy_rs.at[i], device_id=(ia, y_peer(i), it), device_id_type=MESH,
        )

    def cw_copy(i):
        slots = pl.ds(ix * ny, ny)
        return pltpu.make_async_remote_copy(
            src_ref=c4.at[slots], dst_ref=c4.at[slots],
            send_sem=cw_ss.at[i], recv_sem=cw_rs.at[i], device_id=(ia, x_peer(i), it), device_id_type=MESH,
        )

    c3_copy = pltpu.make_async_remote_copy(
        src_ref=c3.at[0], dst_ref=c3.at[1], send_sem=c3_ss, recv_sem=c3_rs,
        device_id=(ia, iw, 1 - it), device_id_type=MESH,
    )

    def start_all(copy):
        def body(i, c):
            copy(h_peer(i), ia).start()
            return c
        lax.fori_loop(1, nh, body, 0)

    def wait_all(copy):
        def body(i, c):
            copy(h_peer(i), h_peer(i)).wait_recv()
            return c
        lax.fori_loop(1, nh, body, 0)

    def wait_sent(copy):
        def body(i, c):
            copy(h_peer(i), ia).wait_send()
            return c
        lax.fori_loop(1, nh, body, 0)

    for i in range(1, nx):
        pa_copy(i).start()

    loads[4].wait()
    cols = 2 * nw
    table = nb.shape[1]
    tiles = [(r - 1, c) for r in range(3) for c in (0, 1)] + [(r - 1, c) for r in range(3) for c in (-1, 2)]
    which = lax.broadcasted_iota(jnp.int32, (16, table), 0)
    numbers = jnp.full((16, table), -5, jnp.int32)
    for n, (r, c) in enumerate(tiles):
        row, col = ia + r, 2 * iw + c
        fine = (row >= 0) & (row < nh) & (col >= 0) & (col < cols)
        numbers = jnp.where(which == n, jnp.where(fine, row * cols + col, -5), numbers)
    chosen = jnp.where(lax.broadcasted_iota(jnp.int32, (16, table), 1) == numbers, 1.0, 0.0)
    lane = lax.broadcasted_iota(jnp.int32, (1, 128), 1)
    for side in range(2):
        hit = jnp.max(jnp.where(nb[...] == ia * cols + 2 * iw + side, 1.0, 0.0), axis=0, keepdims=True)
        hit = jnp.broadcast_to(jnp.max(chosen * hit, axis=1, keepdims=True), (16, 128))
        for b in range(6):
            pen[b, side:side + 1, :] = BIG * (1.0 - jnp.where(lane < 64, hit[2 * b:2 * b + 1], hit[2 * b + 1:2 * b + 2]))

    loads[6].wait()

    def attend(b, c=None, first=False):
        for h in range(heads) if c is None else range(per_chunk * c, per_chunk * (c + 1)):
            hs = slice(HD * h, HD * h + HD)
            k, v, q, g = kv[0, :, hs], kv[1, :, hs], qg[b, 0, :, hs], qg[b, 1, :, hs]
            total = (lro[b, h:h + 1, :] + pen[b, 0:2, :]).reshape(1, 2, 1, 128)
            p = jnp.exp(nt(k, q).reshape(TS, 2, TS, 128) * factor - total).reshape(128, 128)
            ds = (factor * p * (nt(v, g) - lro[b, 8 + h:9 + h, :])).astype(BF16)
            dk, dv = nn(ds, q), nn(p.astype(BF16), g)
            if first:
                dkv_acc[0, :, hs] = dk
                dkv_acc[1, :, hs] = dv
                dqf[b, :, hs] += tn(ds, k)
            else:
                dkv_acc[0, :, hs] += dk
                dkv_acc[1, :, hs] += dv
                dqf[b, :, hs] = tn(ds, k)

    def totals_centre(n):
        lr_copy(n).wait_recv()
        lro[block_of(*STEPS[n])] = lrx[n]

    def totals_outer(west, east):
        lr_copy(west).wait_recv()
        lr_copy(east).wait_recv()
        both = jnp.where(lax.broadcasted_iota(jnp.int32, (16, 128), 1) < 64, lrx[east], lrx[west])
        lro[block_of(*STEPS[west])] = pltpu.roll(both, 64, 1)

    def beside_arrives(c):
        for s in SIDES:
            qg_copy(STEPS.index((0, s)), c).wait_recv()
            for e in SIDES:
                @pl.when(relay_z[e, s])
                def _():
                    forward_z(e, s, c).start()

    def above_below_arrive(c):
        for dr in SIDES:
            qg_copy(STEPS.index((dr, 0)), c).wait_recv()
            for t in SIDES:
                @pl.when(relay_x[dr, t])
                def _():
                    forward_x(dr, t, c).start()

    def send_beside(c, s):
        dq_send[4, rows_of(s), lanes(c)] = dqf[4, rows_of(s), lanes(c)].astype(BF16)
        dq_copy(STEPS.index((0, s)), c).start()

    def attend_beside(c):
        attend(4, c)
        for s in SIDES:
            @pl.when(jnp.logical_not(at_seam[s]))
            def _():
                send_beside(c, s)

    def attend_corners(c):
        for dr in SIDES:
            b = block_of(dr, 1)
            for s in SIDES:
                qg_copy(STEPS.index((dr, s)), c).wait_recv()
            attend(b, c)
            dq_send[b, :, lanes(c)] = dqf[b, :, lanes(c)].astype(BF16)
            for s in SIDES:
                @pl.when(mine[dr, s])
                def _():
                    corner_x(dr, s, c).start()

                @pl.when(jnp.logical_not(mine[dr, s]))
                def _():
                    corner_z(dr, s, c).start()

    def fold(c):
        for s in SIDES:
            for e in SIDES:
                @pl.when(relay_z[e, s])
                def _():
                    corner_z(-e, s, c).wait_recv()
                    dqf[4, rows_of(s), lanes(c)] += cz[bit(e), bit(s), :, lanes(c)].astype(F32)

            @pl.when(at_seam[s])
            def _():
                send_beside(c, s)
        for dr in SIDES:
            for t in SIDES:
                @pl.when(relay_x[dr, t])
                def _():
                    corner_x(dr, -t, c).wait_recv()
                    dqf[dr + 1, rows_of(t), lanes(c)] += cx[bit(dr), bit(t), :, lanes(c)].astype(F32)
            dq_send[dr + 1, :, lanes(c)] = dqf[dr + 1, :, lanes(c)].astype(BF16)
            dq_copy(STEPS.index((dr, 0)), c).start()

    attend(1, first=True)
    totals_outer(2, 3)
    totals_centre(0)
    totals_centre(1)
    for c in range(CHUNKS):
        beside_arrives(c)
        attend_beside(c)
        above_below_arrive(c)
        attend(0, c)
        attend(2, c)
        if c == 0:
            for i in range(1, nx):
                pa_copy(i).wait_recv()
            pa[ix] = ps[pl.ds(ix * ny, ny)]
            for j in range(ny):
                acc = pa[0, j].astype(F32)
                for i in range(1, nx):
                    acc = acc + pa[i, j].astype(F32)
                s1[j] = acc
            for i in range(1, ny):
                pb_copy(i).start()

    for i in range(1, ny):
        pb_copy(i).wait_recv()
    pb[iy] = s1[iy]
    acc = pb[0]
    for j in range(1, ny):
        acc = acc + pb[j]
    t2[...] = jnp.zeros_like(t2)
    for j in range(2 * tr // 8):
        for h in range(heads):
            n = j * heads + h
            t2[n // per_owner, n % per_owner] = acc[8 * j:8 * j + 8, HD * h:HD * h + HD]
    start_all(p2_copy)

    totals_outer(4, 5)
    totals_outer(6, 7)
    attend_corners(0)

    wait_all(p2_copy)
    r2[ia] = t2[ia]
    acc = r2[0]
    for j in range(1, nh):
        acc = acc + r2[j]
    s2[...] = acc
    start_all(p3_copy)

    for c in range(1, CHUNKS):
        attend_corners(c)
    for c in range(CHUNKS):
        fold(c)

    wait_all(p3_copy)
    g2[ia] = s2[...]
    loads[7].wait()
    groups = []
    for j in range(2 * tr // 8):
        tiles = [g2[(j * heads + h) // per_owner, (j * heads + h) % per_owner] for h in range(heads)]
        groups.append(jnp.concatenate(tiles, 1))
    half = len(groups) // 2
    part = nt(jnp.concatenate(groups[:half], 0).astype(BF16), proj[0])
    c3[0] = part + nt(jnp.concatenate(groups[half:], 0).astype(BF16), proj[1])
    c3_copy.start()

    for n in range(2):
        for i in range(4):
            dkv_out[n, 32 * i:32 * i + 32, :] = dkv_acc[n, 32 * i:32 * i + 32, :].astype(BF16)

    c3_copy.wait_recv()
    c4[ix * ny + iy] = c3[0] + c3[1]
    for i in range(1, ny):
        cy_copy(i).start()
    for i in range(1, ny):
        cy_copy(i).wait_recv()
    for i in range(1, nx):
        cw_copy(i).start()

    for c in range(CHUNKS):
        for n in range(4):
            dq_copy(n, c).wait_recv()
    for i in range(4):
        sums = []
        for start in (16 * i, 64 + 16 * i):
            rows = slice(start, start + 16)
            x = dqf[1, rows, :]
            for b in (0, 2, 4):
                x = x + dq_recv[b, rows, :].astype(F32)
            sums.append(x)
        a, b = sums
        dq_out[32 * i:32 * i + 32, :] = jnp.concatenate([a[0:8], b[0:8], a[8:16], b[8:16]], 0).astype(BF16)

    for i in range(1, nx):
        cw_copy(i).wait_recv()
    ctx_out[...] = c4[...].reshape(nw * tr, c4.shape[2]).T

    for c in range(CHUNKS):
        for n in range(4):
            qg_copy(n, c).wait_send()
            dq_copy(n, c).wait_send()
        for a in SIDES:
            for b in SIDES:
                corner_x(a, b, c).wait_send()

                @pl.when(relay_x[a, b])
                def _():
                    forward_x(a, b, c).wait_send()

                @pl.when(relay_z[a, b])
                def _():
                    forward_z(a, b, c).wait_send()
    for n in range(8):
        lr_copy(n).wait_send()
    for i in range(1, nx):
        pa_copy(i).wait_send()
        cw_copy(i).wait_send()
    for i in range(1, ny):
        pb_copy(i).wait_send()
        cy_copy(i).wait_send()
    c3_copy.wait_send()
    wait_sent(p2_copy)
    wait_sent(p3_copy)


def solution(mesh):
    nh, nw = mesh.shape["ha"], mesh.shape["wa"]
    nx = min(RING_X, nw)
    ny = nw // nx

    def local(queries, keys_values, grad_out, log_totals, row_deltas, prompt_kv, prompt_proj, neighbours, prompt_length):
        rows_here, cols_here, width = queries.shape
        heads = log_totals.shape[-1]
        cells = rows_here * cols_here
        text = prompt_kv.shape[1]
        outs = prompt_proj.shape[1]
        tr = text // nw
        count = 2 * tr // 8 * heads
        per_owner = -(-count // nh)
        any_space = pl.BlockSpec(memory_space=pl.ANY)
        vmem = pl.BlockSpec(memory_space=pltpu.VMEM)
        dma = pltpu.SemaphoreType.DMA
        two = lambda n: [dma((n,)), dma((n,))]
        dq, dkv, ctx = pl.pallas_call(
            functools.partial(kernel, nh, nw, heads, per_owner),
            out_shape=(
                jax.ShapeDtypeStruct((cells, width), BF16),
                jax.ShapeDtypeStruct((2, cells, width), BF16),
                jax.ShapeDtypeStruct((outs, text), F32),
            ),
            in_specs=[any_space] * 8 + [pl.BlockSpec(memory_space=pltpu.SMEM)],
            out_specs=(vmem, vmem, vmem),
            scratch_shapes=[
                pltpu.VMEM((cells, width), BF16),
                pltpu.VMEM((2, cells, width), BF16),
                pltpu.VMEM((cells, width), BF16),
                pltpu.VMEM((heads, rows_here, cols_here), F32),
                pltpu.VMEM((heads, rows_here, cols_here), F32),
                pltpu.VMEM((2, text, width), BF16),
                pltpu.VMEM((2, outs, width), BF16),
                pltpu.VMEM(neighbours.shape[::-1], jnp.int32),
                pltpu.VMEM((6, 2, cells, width), BF16),
                pltpu.VMEM((8, 16, cells), F32),
                pltpu.VMEM((6, 16, cells), F32),
                pltpu.VMEM((6, 8, cells), F32),
                pltpu.VMEM((6, cells, width), F32),
                pltpu.VMEM((6, cells, width), BF16),
                pltpu.VMEM((6, cells, width), BF16),
                pltpu.VMEM((2, 2, CELLS, width), BF16),
                pltpu.VMEM((2, 2, CELLS, width), BF16),
                pltpu.VMEM((2, cells, width), F32),
                pltpu.VMEM((nw, 2 * tr, width), BF16),
                pltpu.VMEM((nx, ny, 2 * tr, width), BF16),
                pltpu.VMEM((ny, 2 * tr, width), F32),
                pltpu.VMEM((ny, 2 * tr, width), F32),
                pltpu.VMEM((nh, per_owner, 8, HD), F32),
                pltpu.VMEM((nh, per_owner, 8, HD), F32),
                pltpu.VMEM((per_owner, 8, HD), F32),
                pltpu.VMEM((nh, per_owner, 8, HD), F32),
                pltpu.VMEM((2, tr, outs), F32),
                pltpu.VMEM((nw, tr, outs), F32),
                dma((8,)),
                dma((CHUNKS, 4)), dma((CHUNKS, 8)), dma((CHUNKS, 8)), *two(8),
                dma((CHUNKS, 4)), dma((CHUNKS, 4)), dma((CHUNKS, 4)), dma((CHUNKS, 4)), dma((CHUNKS, 4)),
                *two(nx), *two(ny), *two(nh), *two(nh), dma, dma, *two(ny), *two(nx),
            ],
            compiler_params=pltpu.CompilerParams(
                collective_id=0, has_side_effects=True, vmem_limit_bytes=63 * 2**20
            ),
            name="tile_attention_grads",
        )(
            queries.reshape(cells, width), keys_values.reshape(2, cells, width), grad_out.reshape(cells, width),
            jnp.transpose(log_totals, (2, 0, 1)), jnp.transpose(row_deltas, (2, 0, 1)),
            prompt_kv, prompt_proj, neighbours.T, prompt_length,
        )
        return (
            dq.reshape(rows_here, cols_here, width),
            dkv.reshape(2, rows_here, cols_here, width),
            ctx.T,
        )

    placed = P("ha", "wa", "ta")
    return jax.shard_map(
        local,
        mesh=mesh,
        in_specs=(placed, P(None, "ha", "wa", "ta"), placed, placed, placed, P(None, None, "ta"), P(None, "ha", "ta"), P(), P()),
        out_specs=(placed, P(None, "ha", "wa", "ta"), P(None, "ha")),
        check_vma=False,
    )
```

```python
import functools

import jax
import jax.numpy as jnp
from jax import lax
from jax.experimental import pallas as pl
from jax.experimental.pallas import tpu as pltpu
from jax.sharding import PartitionSpec as P

MESH = pl.DeviceIdType.MESH
F32 = jnp.float32
BF16 = jnp.bfloat16
TS = 8
CELLS = TS * TS
HD = 128
BIG = 1e30
RING_X = 4
RING_Z = 8
CHUNKS = 2
STEPS = [(-1, 0), (1, 0), (0, -1), (0, 1), (-1, -1), (-1, 1), (1, -1), (1, 1)]
SIDES = (-1, 1)


def block_of(row_step, col_step):
    return row_step + 1 if col_step == 0 else row_step + 4


def rows_of(col_step):
    return {0: slice(0, 128), -1: slice(0, 64), 1: slice(64, 128)}[col_step]


def bit(step):
    return (step + 1) // 2


def nt(a, b):
    return lax.dot_general(a, b, (((1,), (1,)), ((), ())), preferred_element_type=F32)


def nn(a, b):
    return lax.dot_general(a, b, (((1,), (0,)), ((), ())), preferred_element_type=F32)


def tn(a, b):
    return lax.dot_general(a, b, (((0,), (0,)), ((), ())), preferred_element_type=F32)


def kernel(
    nh, nw, heads,
    q_hbm, kv_hbm, g_hbm, lt_hbm, rd_hbm, pkv_hbm, proj_hbm, nb_hbm, plen_ref,
    dq_out, dkv_out, ctx_out,
    qn, kv, gn, ltn, rdn, pkv, proj, nb,
    qg, lrx, lro, pen, dqf, dq_send, dq_recv, cx, cz, dkv_acc,
    ps, pa, s1, pb, u1, vz, c3, c4,
    ld_sem, qg_ss, qg_rs, fw_ss, lr_ss, lr_rs, dq_ss, dq_rs, co_ss, cx_rs, cz_rs,
    pa_ss, pa_rs, pb_ss, pb_rs, p2_ss, p2_rs, p3_ss, p3_rs, c3_ss, c3_rs, cy_ss, cy_rs, cw_ss, cw_rs,
):
    width = heads * HD
    nx = min(RING_X, nw)
    ny = nw // nx
    ia, iw, it = lax.axis_index("ha"), lax.axis_index("wa"), lax.axis_index("ta")
    ix, iy = lax.rem(iw, nx), iw // nx
    nz = min(RING_Z, nh)
    nl = nh // nz
    iz, il = lax.rem(ia, nz), ia // nz
    factor = HD ** -0.5
    tr = 128 // nw
    per_chunk = heads // CHUNKS

    def place(row_step, col_step):
        return lax.rem(ia + row_step + nh, nh), lax.rem(iw + col_step + nw, nw)

    def at(row_step, col_step):
        return place(row_step, col_step) + (it,)

    def seam(column, side):
        return lax.rem(column, RING_X) == (0 if side < 0 else RING_X - 1)

    def there(row_step):
        return ia > 0 if row_step < 0 else ia < nh - 1

    def by_x(who, row_step, side):
        return jnp.logical_not(seam(who[1], side))

    def straight(who, row_step, side):
        if row_step == side:
            return ia < 0
        across = lax.rem(who[0], RING_Z) == (0 if row_step < 0 else RING_Z - 1)
        return jnp.logical_and(seam(who[1], side), across)

    def by_z(who, row_step, side):
        return jnp.logical_and(seam(who[1], side), jnp.logical_not(straight(who, row_step, side)))

    def both(a, b):
        return jnp.logical_and(a, b)

    def lanes(c):
        return slice(HD * per_chunk * c, HD * per_chunk * (c + 1))

    barrier = pltpu.get_barrier_semaphore()

    def greet(who):
        pl.semaphore_signal(barrier, inc=1, device_id=who, device_id_type=MESH)

    def x_peer(i):
        return iy * nx + lax.rem(ix + i, nx)

    def y_peer(i):
        return lax.rem(iy + i, ny) * nx + ix

    def l_peer(i):
        return lax.rem(il + i, nl) * nz + iz

    def z_peer(i):
        return il * nz + lax.rem(iz + i, nz)

    for step in STEPS:
        greet(at(*step))
    for i in range(1, nx):
        greet((ia, x_peer(i), it))
    for i in range(1, ny):
        greet((ia, y_peer(i), it))
    for i in range(1, nl):
        greet((l_peer(i), iw, it))
    for i in range(1, nz):
        greet((z_peer(i), iw, it))
    greet((ia, iw, 1 - it))

    loads = [
        pltpu.make_async_copy(src, dst, ld_sem.at[n])
        for n, (src, dst) in enumerate(
            [(q_hbm, qn), (g_hbm, gn), (lt_hbm, ltn), (rd_hbm, rdn), (nb_hbm, nb),
             (pkv_hbm, pkv), (kv_hbm, kv), (proj_hbm, proj)]
        )
    ]
    for load in loads:
        load.start()

    for n, source in ((0, qn), (1, gn)):
        loads[n].wait()
        for i in range(4):
            x = source[32 * i:32 * i + 32, :].astype(F32)
            qg[1, n, 16 * i:16 * i + 16, :] = jnp.concatenate([x[0:8], x[16:24]], 0).astype(BF16)
            qg[1, n, 64 + 16 * i:80 + 16 * i, :] = jnp.concatenate([x[8:16], x[24:32]], 0).astype(BF16)
    for n, source in ((0, ltn), (1, rdn)):
        loads[2 + n].wait()
        pieces = [source[:, r, TS * s:TS * s + TS] for s in (0, 1) for r in range(TS)]
        lro[1, 8 * n:8 * n + heads, :] = jnp.concatenate(pieces, 1)

    pl.semaphore_wait(barrier, 8 + (nx - 1) + (ny - 1) + (nl - 1) + (nz - 1) + 1)

    def qg_copy(n, c):
        dr, dc = STEPS[n]
        return pltpu.make_async_remote_copy(
            src_ref=qg.at[1, :, rows_of(-dc), lanes(c)],
            dst_ref=qg.at[block_of(dr, dc), :, rows_of(dc), lanes(c)],
            send_sem=qg_ss.at[c, n], recv_sem=qg_rs.at[c, n],
            device_id=at(-dr, -dc), device_id_type=MESH,
        )

    def forward_x(dr, t, c):
        return pltpu.make_async_remote_copy(
            src_ref=qg.at[block_of(dr, 0), :, rows_of(t), lanes(c)],
            dst_ref=qg.at[block_of(dr, -t), :, rows_of(-t), lanes(c)],
            send_sem=fw_ss.at[c, 2 * bit(dr) + bit(t)], recv_sem=qg_rs.at[c, STEPS.index((dr, -t))],
            device_id=at(0, t), device_id_type=MESH,
        )

    def forward_z(e, s, c):
        return pltpu.make_async_remote_copy(
            src_ref=qg.at[block_of(0, s), :, rows_of(s), lanes(c)],
            dst_ref=qg.at[block_of(-e, s), :, rows_of(s), lanes(c)],
            send_sem=fw_ss.at[c, 4 + 2 * bit(e) + bit(s)], recv_sem=qg_rs.at[c, STEPS.index((-e, s))],
            device_id=at(e, 0), device_id_type=MESH,
        )

    def lr_copy(n):
        dr, dc = STEPS[n]
        return pltpu.make_async_remote_copy(
            src_ref=lro.at[1], dst_ref=lrx.at[n],
            send_sem=lr_ss.at[n], recv_sem=lr_rs.at[n],
            device_id=at(-dr, -dc), device_id_type=MESH,
        )

    def dq_copy(n, c):
        dr, dc = STEPS[n]
        return pltpu.make_async_remote_copy(
            src_ref=dq_send.at[block_of(dr, dc), rows_of(dc), lanes(c)],
            dst_ref=dq_recv.at[block_of(-dr, -dc), rows_of(-dc), lanes(c)],
            send_sem=dq_ss.at[c, n], recv_sem=dq_rs.at[c, n],
            device_id=at(dr, dc), device_id_type=MESH,
        )

    def corner_x(dr, s, c):
        return pltpu.make_async_remote_copy(
            src_ref=dq_send.at[block_of(dr, s), rows_of(s), lanes(c)],
            dst_ref=cx.at[bit(dr), bit(-s), :, lanes(c)],
            send_sem=co_ss.at[c, 2 * bit(dr) + bit(s)], recv_sem=cx_rs.at[c, 2 * bit(dr) + bit(-s)],
            device_id=at(0, s), device_id_type=MESH,
        )

    def corner_z(dr, s, c):
        return pltpu.make_async_remote_copy(
            src_ref=dq_send.at[block_of(dr, s), rows_of(s), lanes(c)],
            dst_ref=cz.at[bit(-dr), bit(s), :, lanes(c)],
            send_sem=co_ss.at[c, 2 * bit(dr) + bit(s)], recv_sem=cz_rs.at[c, 2 * bit(-dr) + bit(s)],
            device_id=at(dr, 0), device_id_type=MESH,
        )

    pairs = [(a, b) for a in SIDES for b in SIDES]
    has = {dr: there(dr) for dr in SIDES}
    mine_x = {(dr, s): both(has[dr], by_x((ia, iw), dr, s)) for dr, s in pairs}
    mine_z = {(dr, s): both(has[dr], by_z((ia, iw), dr, s)) for dr, s in pairs}
    mine_s = {(dr, s): both(has[dr], straight((ia, iw), dr, s)) for dr, s in pairs}
    relay_x = {(dr, t): both(has[dr], by_x(place(0, t), dr, -t)) for dr, t in pairs}
    relay_z = {(e, s): both(has[e], by_z(place(e, 0), -e, s)) for e, s in pairs}
    to_s = {(a, b): both(has[a], straight(place(a, b), -a, -b)) for a, b in pairs}
    at_seam = {s: seam(iw, s) for s in SIDES}
    diagonal = [(a, b) for a, b in pairs if a != b]

    for n in range(8):
        lr_copy(n).start()
    for c in range(CHUNKS):
        for s in SIDES:
            qg_copy(STEPS.index((0, s)), c).start()
        for dr in SIDES:
            @pl.when(has[-dr])
            def _():
                qg_copy(STEPS.index((dr, 0)), c).start()
        for a, b in diagonal:
            @pl.when(to_s[a, b])
            def _():
                qg_copy(STEPS.index((-a, -b)), c).start()
    for dr in SIDES:
        @pl.when(jnp.logical_not(has[dr]))
        def _():
            qg[dr + 1] = jnp.zeros(qg.shape[1:], BF16)
            qg[dr + 4] = jnp.zeros(qg.shape[1:], BF16)
            dq_recv[dr + 1] = jnp.zeros(dq_recv.shape[1:], BF16)
    loads[5].wait()
    live = lax.broadcasted_iota(jnp.int32, (128, 128), 0) < plen_ref[0]
    for h in range(heads):
        hs = slice(HD * h, HD * h + HD)
        k, v, q, g = pkv[0, :, hs], pkv[1, :, hs], qg[1, 0, :, hs], qg[1, 1, :, hs]
        p = jnp.exp(jnp.where(live, nt(k, q) * factor - lro[1, h:h + 1, :], -BIG))
        ds = (factor * p * (nt(v, g) - lro[1, 8 + h:9 + h, :])).astype(BF16)
        dk = nn(ds, q).reshape(nw, tr, HD)
        dv = nn(p.astype(BF16), g).reshape(nw, tr, HD)
        ps[:, :, hs] = jnp.concatenate([dk, dv], 1).astype(BF16)
        dqf[1, :, hs] = tn(ds, k)

    def pa_copy(i):
        return pltpu.make_async_remote_copy(
            src_ref=ps.at[pl.ds(lax.rem(ix + i, nx) * ny, ny)], dst_ref=pa.at[ix],
            send_sem=pa_ss.at[i], recv_sem=pa_rs.at[i], device_id=(ia, x_peer(i), it), device_id_type=MESH,
        )

    def pb_copy(i):
        return pltpu.make_async_remote_copy(
            src_ref=s1.at[lax.rem(iy + i, ny)], dst_ref=pb.at[iy],
            send_sem=pb_ss.at[i], recv_sem=pb_rs.at[i], device_id=(ia, y_peer(i), it), device_id_type=MESH,
        )

    def p2_copy(i):
        return pltpu.make_async_remote_copy(
            src_ref=u1.at[il], dst_ref=u1.at[il], send_sem=p2_ss.at[i],
            recv_sem=p2_rs.at[i], device_id=(l_peer(i), iw, it), device_id_type=MESH,
        )

    def p3_copy(i):
        return pltpu.make_async_remote_copy(
            src_ref=vz.at[iz], dst_ref=vz.at[iz], send_sem=p3_ss.at[i],
            recv_sem=p3_rs.at[i], device_id=(z_peer(i), iw, it), device_id_type=MESH,
        )

    def cy_copy(i):
        own_slot = ix * ny + iy
        return pltpu.make_async_remote_copy(
            src_ref=c4.at[own_slot], dst_ref=c4.at[own_slot],
            send_sem=cy_ss.at[i], recv_sem=cy_rs.at[i], device_id=(ia, y_peer(i), it), device_id_type=MESH,
        )

    def cw_copy(i):
        slots = pl.ds(ix * ny, ny)
        return pltpu.make_async_remote_copy(
            src_ref=c4.at[slots], dst_ref=c4.at[slots],
            send_sem=cw_ss.at[i], recv_sem=cw_rs.at[i], device_id=(ia, x_peer(i), it), device_id_type=MESH,
        )

    c3_copy = pltpu.make_async_remote_copy(
        src_ref=c3.at[0], dst_ref=c3.at[1], send_sem=c3_ss, recv_sem=c3_rs,
        device_id=(ia, iw, 1 - it), device_id_type=MESH,
    )

    for i in range(1, nx):
        pa_copy(i).start()

    loads[4].wait()
    cols = 2 * nw
    table = nb.shape[1]
    tiles = [(r - 1, c) for r in range(3) for c in (0, 1)] + [(r - 1, c) for r in range(3) for c in (-1, 2)]
    which = lax.broadcasted_iota(jnp.int32, (16, table), 0)
    numbers = jnp.full((16, table), -5, jnp.int32)
    for n, (r, c) in enumerate(tiles):
        row, col = ia + r, 2 * iw + c
        fine = (row >= 0) & (row < nh) & (col >= 0) & (col < cols)
        numbers = jnp.where(which == n, jnp.where(fine, row * cols + col, -5), numbers)
    chosen = jnp.where(lax.broadcasted_iota(jnp.int32, (16, table), 1) == numbers, 1.0, 0.0)
    lane = lax.broadcasted_iota(jnp.int32, (1, 128), 1)
    for side in range(2):
        hit = jnp.max(jnp.where(nb[...] == ia * cols + 2 * iw + side, 1.0, 0.0), axis=0, keepdims=True)
        hit = jnp.broadcast_to(jnp.max(chosen * hit, axis=1, keepdims=True), (16, 128))
        for b in range(6):
            pen[b, side:side + 1, :] = BIG * (1.0 - jnp.where(lane < 64, hit[2 * b:2 * b + 1], hit[2 * b + 1:2 * b + 2]))

    loads[6].wait()

    def attend(b, c=None, first=False):
        for h in range(heads) if c is None else range(per_chunk * c, per_chunk * (c + 1)):
            hs = slice(HD * h, HD * h + HD)
            k, v, q, g = kv[0, :, hs], kv[1, :, hs], qg[b, 0, :, hs], qg[b, 1, :, hs]
            total = (lro[b, h:h + 1, :] + pen[b, 0:2, :]).reshape(1, 2, 1, 128)
            p = jnp.exp(nt(k, q).reshape(TS, 2, TS, 128) * factor - total).reshape(128, 128)
            ds = (factor * p * (nt(v, g) - lro[b, 8 + h:9 + h, :])).astype(BF16)
            dk, dv = nn(ds, q), nn(p.astype(BF16), g)
            if first:
                dkv_acc[0, :, hs] = dk
                dkv_acc[1, :, hs] = dv
                dqf[b, :, hs] += tn(ds, k)
            else:
                dkv_acc[0, :, hs] += dk
                dkv_acc[1, :, hs] += dv
                dqf[b, :, hs] = tn(ds, k)

    def totals_centre(n):
        lr_copy(n).wait_recv()
        lro[block_of(*STEPS[n])] = lrx[n]

    def totals_outer(west, east):
        lr_copy(west).wait_recv()
        lr_copy(east).wait_recv()
        both = jnp.where(lax.broadcasted_iota(jnp.int32, (16, 128), 1) < 64, lrx[east], lrx[west])
        lro[block_of(*STEPS[west])] = pltpu.roll(both, 64, 1)

    def beside_arrives(c):
        for s in SIDES:
            qg_copy(STEPS.index((0, s)), c).wait_recv()
            for e in SIDES:
                @pl.when(relay_z[e, s])
                def _():
                    forward_z(e, s, c).start()

    def above_below_arrive(c):
        for dr in SIDES:
            @pl.when(has[dr])
            def _():
                qg_copy(STEPS.index((dr, 0)), c).wait_recv()
            for t in SIDES:
                @pl.when(relay_x[dr, t])
                def _():
                    forward_x(dr, t, c).start()

    def send_beside(c, s):
        dq_send[4, rows_of(s), lanes(c)] = dqf[4, rows_of(s), lanes(c)].astype(BF16)
        dq_copy(STEPS.index((0, s)), c).start()

    def attend_beside(c):
        attend(4, c)
        for s in SIDES:
            @pl.when(jnp.logical_not(at_seam[s]))
            def _():
                send_beside(c, s)

    def attend_corners(c):
        for dr in SIDES:
            b = block_of(dr, 1)
            for s in SIDES:
                @pl.when(has[dr])
                def _():
                    qg_copy(STEPS.index((dr, s)), c).wait_recv()
            attend(b, c)
            dq_send[b, :, lanes(c)] = dqf[b, :, lanes(c)].astype(BF16)
            for s in SIDES:
                @pl.when(mine_x[dr, s])
                def _():
                    corner_x(dr, s, c).start()

                @pl.when(mine_z[dr, s])
                def _():
                    corner_z(dr, s, c).start()

                if (dr, s) in diagonal:
                    @pl.when(mine_s[dr, s])
                    def _():
                        dq_copy(STEPS.index((dr, s)), c).start()

    def fold(c):
        for s in SIDES:
            for e in SIDES:
                @pl.when(relay_z[e, s])
                def _():
                    corner_z(-e, s, c).wait_recv()
                    dqf[4, rows_of(s), lanes(c)] += cz[bit(e), bit(s), :, lanes(c)].astype(F32)

            @pl.when(at_seam[s])
            def _():
                send_beside(c, s)
        for dr in SIDES:
            for t in SIDES:
                @pl.when(relay_x[dr, t])
                def _():
                    corner_x(dr, -t, c).wait_recv()
                    dqf[dr + 1, rows_of(t), lanes(c)] += cx[bit(dr), bit(t), :, lanes(c)].astype(F32)
            dq_send[dr + 1, :, lanes(c)] = dqf[dr + 1, :, lanes(c)].astype(BF16)

            @pl.when(has[dr])
            def _():
                dq_copy(STEPS.index((dr, 0)), c).start()

    def sum_over_x():
        for i in range(1, nx):
            pa_copy(i).wait_recv()
        pa[ix] = ps[pl.ds(ix * ny, ny)]
        for j in range(ny):
            acc = pa[0, j].astype(F32)
            for i in range(1, nx):
                acc = acc + pa[i, j].astype(F32)
            s1[j] = acc
        for i in range(1, ny):
            pb_copy(i).start()

    def sum_over_y():
        for i in range(1, ny):
            pb_copy(i).wait_recv()
        pb[iy] = s1[iy]
        acc = pb[0]
        for j in range(1, ny):
            acc = acc + pb[j]
        u1[il] = acc
        for i in range(1, nl):
            p2_copy(i).start()

    def sum_over_rows():
        for i in range(1, nl):
            p2_copy(i).wait_recv()
        acc = u1[0]
        for j in range(1, nl):
            acc = acc + u1[j]
        vz[iz] = acc.astype(BF16)
        for i in range(1, nz):
            p3_copy(i).start()

    def project():
        for i in range(1, nz):
            p3_copy(i).wait_recv()
        loads[7].wait()
        acc = vz[0].astype(F32)
        for j in range(1, nz):
            acc = acc + vz[j].astype(F32)
        acc = acc.astype(BF16)
        c3[0] = nt(acc[:tr], proj[0]) + nt(acc[tr:], proj[1])
        c3_copy.start()

    def gather_over_y():
        c3_copy.wait_recv()
        c4[ix * ny + iy] = c3[0] + c3[1]
        for i in range(1, ny):
            cy_copy(i).start()

    def gather_over_x():
        for i in range(1, ny):
            cy_copy(i).wait_recv()
        for i in range(1, nx):
            cw_copy(i).start()

    def write_context():
        for i in range(1, nx):
            cw_copy(i).wait_recv()
        ctx_out[...] = c4[...].reshape(nw * tr, c4.shape[2]).T

    def write_keys():
        for n in range(2):
            for i in range(4):
                dkv_out[n, 32 * i:32 * i + 32, :] = dkv_acc[n, 32 * i:32 * i + 32, :].astype(BF16)

    def write_queries():
        for c in range(CHUNKS):
            for s in SIDES:
                dq_copy(STEPS.index((0, s)), c).wait_recv()
            for dr in SIDES:
                @pl.when(has[-dr])
                def _():
                    dq_copy(STEPS.index((dr, 0)), c).wait_recv()
            for a, b in diagonal:
                @pl.when(to_s[a, b])
                def _():
                    dq_copy(STEPS.index((-a, -b)), c).wait_recv()
                    dqf[1, rows_of(b), lanes(c)] += dq_recv[block_of(a, b), rows_of(b), lanes(c)].astype(F32)
        for i in range(4):
            sums = []
            for start in (16 * i, 64 + 16 * i):
                rows = slice(start, start + 16)
                x = dqf[1, rows, :]
                for b in (0, 2, 4):
                    x = x + dq_recv[b, rows, :].astype(F32)
                sums.append(x)
            a, b = sums
            dq_out[32 * i:32 * i + 32, :] = jnp.concatenate([a[0:8], b[0:8], a[8:16], b[8:16]], 0).astype(BF16)

    attend(1, first=True)
    totals_outer(2, 3)
    beside_arrives(0)
    sum_over_x()
    for c in range(1, CHUNKS):
        beside_arrives(c)
    totals_centre(0)
    totals_centre(1)
    above_below_arrive(0)
    attend_beside(0)
    sum_over_y()
    for c in range(1, CHUNKS):
        above_below_arrive(c)
    for c in range(1, CHUNKS):
        attend_beside(c)
    attend(0, 0)
    attend(2, 0)
    sum_over_rows()
    for c in range(1, CHUNKS):
        attend(0, c)
        attend(2, c)
    totals_outer(4, 5)
    totals_outer(6, 7)
    attend_corners(0)
    project()
    for c in range(1, CHUNKS):
        attend_corners(c)
    gather_over_y()
    for c in range(CHUNKS):
        fold(c)
    write_keys()
    gather_over_x()
    write_queries()
    write_context()

    for c in range(CHUNKS):
        for s in SIDES:
            qg_copy(STEPS.index((0, s)), c).wait_send()
            dq_copy(STEPS.index((0, s)), c).wait_send()

            @pl.when(has[-s])
            def _():
                qg_copy(STEPS.index((s, 0)), c).wait_send()

            @pl.when(has[s])
            def _():
                dq_copy(STEPS.index((s, 0)), c).wait_send()
        for a, b in diagonal:
            @pl.when(to_s[a, b])
            def _():
                qg_copy(STEPS.index((-a, -b)), c).wait_send()

            @pl.when(mine_s[a, b])
            def _():
                dq_copy(STEPS.index((a, b)), c).wait_send()
        for a, b in pairs:
            @pl.when(both(has[a], jnp.logical_not(mine_s[a, b])))
            def _():
                corner_x(a, b, c).wait_send()

            @pl.when(relay_x[a, b])
            def _():
                forward_x(a, b, c).wait_send()

            @pl.when(relay_z[a, b])
            def _():
                forward_z(a, b, c).wait_send()
    for n in range(8):
        lr_copy(n).wait_send()
    for i in range(1, nx):
        pa_copy(i).wait_send()
        cw_copy(i).wait_send()
    for i in range(1, ny):
        pb_copy(i).wait_send()
        cy_copy(i).wait_send()
    c3_copy.wait_send()
    for i in range(1, nl):
        p2_copy(i).wait_send()
    for i in range(1, nz):
        p3_copy(i).wait_send()


def solution(mesh):
    nh, nw = mesh.shape["ha"], mesh.shape["wa"]
    nx = min(RING_X, nw)
    ny = nw // nx
    nz = min(RING_Z, nh)
    nl = nh // nz

    def local(queries, keys_values, grad_out, log_totals, row_deltas, prompt_kv, prompt_proj, neighbours, prompt_length):
        rows_here, cols_here, width = queries.shape
        heads = log_totals.shape[-1]
        cells = rows_here * cols_here
        text = prompt_kv.shape[1]
        outs = prompt_proj.shape[1]
        tr = text // nw
        any_space = pl.BlockSpec(memory_space=pl.ANY)
        vmem = pl.BlockSpec(memory_space=pltpu.VMEM)
        dma = pltpu.SemaphoreType.DMA
        two = lambda n: [dma((n,)), dma((n,))]
        dq, dkv, ctx = pl.pallas_call(
            functools.partial(kernel, nh, nw, heads),
            out_shape=(
                jax.ShapeDtypeStruct((cells, width), BF16),
                jax.ShapeDtypeStruct((2, cells, width), BF16),
                jax.ShapeDtypeStruct((outs, text), F32),
            ),
            in_specs=[any_space] * 8 + [pl.BlockSpec(memory_space=pltpu.SMEM)],
            out_specs=(vmem, vmem, vmem),
            scratch_shapes=[
                pltpu.VMEM((cells, width), BF16),
                pltpu.VMEM((2, cells, width), BF16),
                pltpu.VMEM((cells, width), BF16),
                pltpu.VMEM((heads, rows_here, cols_here), F32),
                pltpu.VMEM((heads, rows_here, cols_here), F32),
                pltpu.VMEM((2, text, width), BF16),
                pltpu.VMEM((2, outs, width), BF16),
                pltpu.VMEM(neighbours.shape[::-1], jnp.int32),
                pltpu.VMEM((6, 2, cells, width), BF16),
                pltpu.VMEM((8, 16, cells), F32),
                pltpu.VMEM((6, 16, cells), F32),
                pltpu.VMEM((6, 8, cells), F32),
                pltpu.VMEM((6, cells, width), F32),
                pltpu.VMEM((6, cells, width), BF16),
                pltpu.VMEM((6, cells, width), BF16),
                pltpu.VMEM((2, 2, CELLS, width), BF16),
                pltpu.VMEM((2, 2, CELLS, width), BF16),
                pltpu.VMEM((2, cells, width), F32),
                pltpu.VMEM((nw, 2 * tr, width), BF16),
                pltpu.VMEM((nx, ny, 2 * tr, width), BF16),
                pltpu.VMEM((ny, 2 * tr, width), F32),
                pltpu.VMEM((ny, 2 * tr, width), F32),
                pltpu.VMEM((nl, 2 * tr, width), F32),
                pltpu.VMEM((nz, 2 * tr, width), BF16),
                pltpu.VMEM((2, tr, outs), F32),
                pltpu.VMEM((nw, tr, outs), F32),
                dma((8,)),
                dma((CHUNKS, 8)), dma((CHUNKS, 8)), dma((CHUNKS, 8)), *two(8),
                dma((CHUNKS, 8)), dma((CHUNKS, 8)), dma((CHUNKS, 4)), dma((CHUNKS, 4)), dma((CHUNKS, 4)),
                *two(nx), *two(ny), *two(nl), *two(nz), dma, dma, *two(ny), *two(nx),
            ],
            compiler_params=pltpu.CompilerParams(
                collective_id=0, has_side_effects=True, vmem_limit_bytes=63 * 2**20
            ),
            name="tile_attention_grads",
        )(
            queries.reshape(cells, width), keys_values.reshape(2, cells, width), grad_out.reshape(cells, width),
            jnp.transpose(log_totals, (2, 0, 1)), jnp.transpose(row_deltas, (2, 0, 1)),
            prompt_kv, prompt_proj, neighbours.T, prompt_length,
        )
        return (
            dq.reshape(rows_here, cols_here, width),
            dkv.reshape(2, rows_here, cols_here, width),
            ctx.T,
        )

    placed = P("ha", "wa", "ta")
    return jax.shard_map(
        local,
        mesh=mesh,
        in_specs=(placed, P(None, "ha", "wa", "ta"), placed, placed, placed, P(None, None, "ta"), P(None, "ha", "ta"), P(), P()),
        out_specs=(placed, P(None, "ha", "wa", "ta"), P(None, "ha")),
        check_vma=False,
    )
```

```python
import functools

import jax
import jax.numpy as jnp
from jax import lax
from jax.experimental import pallas as pl
from jax.experimental.pallas import tpu as pltpu
from jax.sharding import PartitionSpec as P

MESH = pl.DeviceIdType.MESH
F32 = jnp.float32
BF16 = jnp.bfloat16
TS = 8
CELLS = TS * TS
HD = 128
BIG = 1e30
RING_X = 4
RING_Z = 8
CHUNKS = 2
STEPS = [(-1, 0), (1, 0), (0, -1), (0, 1), (-1, -1), (-1, 1), (1, -1), (1, 1)]
SIDES = (-1, 1)


def block_of(row_step, col_step):
    return row_step + 1 if col_step == 0 else row_step + 4


def rows_of(col_step):
    return {0: slice(0, 128), -1: slice(0, 64), 1: slice(64, 128)}[col_step]


def bit(step):
    return (step + 1) // 2


def nt(a, b):
    return lax.dot_general(a, b, (((1,), (1,)), ((), ())), preferred_element_type=F32)


def nn(a, b):
    return lax.dot_general(a, b, (((1,), (0,)), ((), ())), preferred_element_type=F32)


def tn(a, b):
    return lax.dot_general(a, b, (((0,), (0,)), ((), ())), preferred_element_type=F32)


def kernel(
    nh, nw, heads,
    q_hbm, kv_hbm, g_hbm, lt_hbm, rd_hbm, pkv_hbm, proj_hbm, nb_hbm, plen_ref,
    dq_out, dkv_out, ctx_out,
    qn, kv, gn, ltn, rdn, pkv, proj, nb,
    qg, held, lrx, lro, pen, dqf, dq_send, dq_recv, cx, cz, dkv_acc,
    ps, pa, s1, pb, u1, vz, c3, c4,
    ld_sem, qg_ss, qg_rs, fw_ss, hp_ss, hp_rs, hf_ss, lr_ss, lr_rs, dq_ss, dq_rs, co_ss, cx_rs, cz_rs,
    pa_ss, pa_rs, pb_ss, pb_rs, p2_ss, p2_rs, p3_ss, p3_rs, c3_ss, c3_rs, cy_ss, cy_rs, cw_ss, cw_rs,
):
    width = heads * HD
    nx = min(RING_X, nw)
    ny = nw // nx
    ia, iw, it = lax.axis_index("ha"), lax.axis_index("wa"), lax.axis_index("ta")
    ix, iy = lax.rem(iw, nx), iw // nx
    nz = min(RING_Z, nh)
    nl = nh // nz
    iz, il = lax.rem(ia, nz), ia // nz
    factor = HD ** -0.5
    tr = 128 // nw
    per_chunk = heads // CHUNKS

    def place(row_step, col_step):
        return lax.rem(ia + row_step + nh, nh), lax.rem(iw + col_step + nw, nw)

    def at(row_step, col_step):
        return place(row_step, col_step) + (it,)

    def seam(column, side):
        return lax.rem(column, RING_X) == (0 if side < 0 else RING_X - 1)

    def there(row_step):
        return ia > 0 if row_step < 0 else ia < nh - 1

    def by_x(who, row_step, side):
        return jnp.logical_not(seam(who[1], side))

    def straight(who, row_step, side):
        if row_step == side:
            return ia < 0
        across = lax.rem(who[0], RING_Z) == (0 if row_step < 0 else RING_Z - 1)
        return jnp.logical_and(seam(who[1], side), across)

    def by_z(who, row_step, side):
        return jnp.logical_and(seam(who[1], side), jnp.logical_not(straight(who, row_step, side)))

    def both(a, b):
        return jnp.logical_and(a, b)

    def lanes(c):
        return slice(HD * per_chunk * c, HD * per_chunk * (c + 1))

    barrier = pltpu.get_barrier_semaphore()

    def greet(who):
        pl.semaphore_signal(barrier, inc=1, device_id=who, device_id_type=MESH)

    def x_peer(i):
        return iy * nx + lax.rem(ix + i, nx)

    def y_peer(i):
        return lax.rem(iy + i, ny) * nx + ix

    def l_peer(i):
        return lax.rem(il + i, nl) * nz + iz

    def z_peer(i):
        return il * nz + lax.rem(iz + i, nz)

    for step in STEPS:
        greet(at(*step))
    for i in range(1, nx):
        greet((ia, x_peer(i), it))
    for i in range(1, ny):
        greet((ia, y_peer(i), it))
    for i in range(1, nl):
        greet((l_peer(i), iw, it))
    for i in range(1, nz):
        greet((z_peer(i), iw, it))
    greet((ia, iw, 1 - it))

    loads = [
        pltpu.make_async_copy(src, dst, ld_sem.at[n])
        for n, (src, dst) in enumerate(
            [(q_hbm, qn), (g_hbm, gn), (lt_hbm, ltn), (rd_hbm, rdn), (nb_hbm, nb),
             (pkv_hbm, pkv), (kv_hbm, kv), (proj_hbm, proj)]
        )
    ]
    for load in loads:
        load.start()

    for n, source in ((0, qn), (1, gn)):
        loads[n].wait()
        for i in range(4):
            x = source[32 * i:32 * i + 32, :].astype(F32)
            qg[1, n, 16 * i:16 * i + 16, :] = jnp.concatenate([x[0:8], x[16:24]], 0).astype(BF16)
            qg[1, n, 64 + 16 * i:80 + 16 * i, :] = jnp.concatenate([x[8:16], x[24:32]], 0).astype(BF16)
    for n, source in ((0, ltn), (1, rdn)):
        loads[2 + n].wait()
        pieces = [source[:, r, TS * s:TS * s + TS] for s in (0, 1) for r in range(TS)]
        lro[1, 8 * n:8 * n + heads, :] = jnp.concatenate(pieces, 1)

    pl.semaphore_wait(barrier, 8 + (nx - 1) + (ny - 1) + (nl - 1) + (nz - 1) + 1)

    def qg_copy(n, c):
        dr, dc = STEPS[n]
        return pltpu.make_async_remote_copy(
            src_ref=qg.at[1, :, rows_of(-dc), lanes(c)],
            dst_ref=qg.at[block_of(dr, dc), :, rows_of(dc), lanes(c)],
            send_sem=qg_ss.at[c, n], recv_sem=qg_rs.at[c, n],
            device_id=at(-dr, -dc), device_id_type=MESH,
        )

    def forward_x(dr, t, c):
        return pltpu.make_async_remote_copy(
            src_ref=qg.at[block_of(dr, 0), :, rows_of(t), lanes(c)],
            dst_ref=qg.at[block_of(dr, -t), :, rows_of(-t), lanes(c)],
            send_sem=fw_ss.at[c, 2 * bit(dr) + bit(t)], recv_sem=qg_rs.at[c, STEPS.index((dr, -t))],
            device_id=at(0, t), device_id_type=MESH,
        )

    def forward_z(e, s, c):
        return pltpu.make_async_remote_copy(
            src_ref=qg.at[block_of(0, s), :, rows_of(s), lanes(c)],
            dst_ref=qg.at[block_of(-e, s), :, rows_of(s), lanes(c)],
            send_sem=fw_ss.at[c, 4 + 2 * bit(e) + bit(s)], recv_sem=qg_rs.at[c, STEPS.index((-e, s))],
            device_id=at(e, 0), device_id_type=MESH,
        )

    def hop_copy(dr):
        return pltpu.make_async_remote_copy(
            src_ref=qg.at[1, :, :, lanes(CHUNKS - 1)], dst_ref=held.at[bit(dr)],
            send_sem=hp_ss.at[bit(dr)], recv_sem=hp_rs.at[bit(dr)],
            device_id=(il * nz + lax.rem(iz - dr + nz, nz), iw, it), device_id_type=MESH,
        )

    def hop_forward(dr):
        return pltpu.make_async_remote_copy(
            src_ref=held.at[bit(dr)], dst_ref=qg.at[block_of(dr, 0), :, :, lanes(CHUNKS - 1)],
            send_sem=hf_ss.at[bit(dr)], recv_sem=qg_rs.at[CHUNKS - 1, STEPS.index((dr, 0))],
            device_id=(lax.rem(ia - dr * nz + nh, nh), iw, it), device_id_type=MESH,
        )

    def lr_copy(n):
        dr, dc = STEPS[n]
        return pltpu.make_async_remote_copy(
            src_ref=lro.at[1], dst_ref=lrx.at[n],
            send_sem=lr_ss.at[n], recv_sem=lr_rs.at[n],
            device_id=at(-dr, -dc), device_id_type=MESH,
        )

    def dq_copy(n, c):
        dr, dc = STEPS[n]
        return pltpu.make_async_remote_copy(
            src_ref=dq_send.at[block_of(dr, dc), rows_of(dc), lanes(c)],
            dst_ref=dq_recv.at[block_of(-dr, -dc), rows_of(-dc), lanes(c)],
            send_sem=dq_ss.at[c, n], recv_sem=dq_rs.at[c, n],
            device_id=at(dr, dc), device_id_type=MESH,
        )

    def corner_x(dr, s, c):
        return pltpu.make_async_remote_copy(
            src_ref=dq_send.at[block_of(dr, s), rows_of(s), lanes(c)],
            dst_ref=cx.at[bit(dr), bit(-s), :, lanes(c)],
            send_sem=co_ss.at[c, 2 * bit(dr) + bit(s)], recv_sem=cx_rs.at[c, 2 * bit(dr) + bit(-s)],
            device_id=at(0, s), device_id_type=MESH,
        )

    def corner_z(dr, s, c):
        return pltpu.make_async_remote_copy(
            src_ref=dq_send.at[block_of(dr, s), rows_of(s), lanes(c)],
            dst_ref=cz.at[bit(-dr), bit(s), :, lanes(c)],
            send_sem=co_ss.at[c, 2 * bit(dr) + bit(s)], recv_sem=cz_rs.at[c, 2 * bit(-dr) + bit(s)],
            device_id=at(dr, 0), device_id_type=MESH,
        )

    pairs = [(a, b) for a in SIDES for b in SIDES]
    has = {dr: there(dr) for dr in SIDES}
    mine_x = {(dr, s): both(has[dr], by_x((ia, iw), dr, s)) for dr, s in pairs}
    mine_z = {(dr, s): both(has[dr], by_z((ia, iw), dr, s)) for dr, s in pairs}
    mine_s = {(dr, s): both(has[dr], straight((ia, iw), dr, s)) for dr, s in pairs}
    relay_x = {(dr, t): both(has[dr], by_x(place(0, t), dr, -t)) for dr, t in pairs}
    relay_z = {(e, s): both(has[e], by_z(place(e, 0), -e, s)) for e, s in pairs}
    to_s = {(a, b): both(has[a], straight(place(a, b), -a, -b)) for a, b in pairs}
    at_seam = {s: seam(iw, s) for s in SIDES}
    crowded = {-1: ix == nx - 1, 1: ix == 0}
    hops = {
        -1: both(crowded[-1], both(iz == nz - 1, has[1])),
        1: both(crowded[1], both(iz == 0, has[-1])),
    }
    relays = {
        -1: both(crowded[-1], both(iz == 0, ia + nz < nh)),
        1: both(crowded[1], both(iz == nz - 1, ia >= nz)),
    }
    passes = {dr: both(has[-dr], jnp.logical_not(hops[dr])) for dr in SIDES}
    diagonal = [(a, b) for a, b in pairs if a != b]

    for n in range(8):
        lr_copy(n).start()
    for c in range(CHUNKS):
        for s in SIDES:
            qg_copy(STEPS.index((0, s)), c).start()
        for dr in SIDES:
            @pl.when(passes[dr] if c == CHUNKS - 1 else has[-dr])
            def _():
                qg_copy(STEPS.index((dr, 0)), c).start()

            if c == CHUNKS - 1:
                @pl.when(hops[dr])
                def _():
                    hop_copy(dr).start()
        for a, b in diagonal:
            @pl.when(to_s[a, b])
            def _():
                qg_copy(STEPS.index((-a, -b)), c).start()
    for dr in SIDES:
        @pl.when(jnp.logical_not(has[dr]))
        def _():
            qg[dr + 1] = jnp.zeros(qg.shape[1:], BF16)
            qg[dr + 4] = jnp.zeros(qg.shape[1:], BF16)
            dq_recv[dr + 1] = jnp.zeros(dq_recv.shape[1:], BF16)
    loads[5].wait()
    live = lax.broadcasted_iota(jnp.int32, (128, 128), 0) < plen_ref[0]
    for h in range(heads):
        hs = slice(HD * h, HD * h + HD)
        k, v, q, g = pkv[0, :, hs], pkv[1, :, hs], qg[1, 0, :, hs], qg[1, 1, :, hs]
        p = jnp.exp(jnp.where(live, nt(k, q) * factor - lro[1, h:h + 1, :], -BIG))
        ds = (factor * p * (nt(v, g) - lro[1, 8 + h:9 + h, :])).astype(BF16)
        dk = nn(ds, q).reshape(nw, tr, HD)
        dv = nn(p.astype(BF16), g).reshape(nw, tr, HD)
        ps[:, :, hs] = jnp.concatenate([dk, dv], 1).astype(BF16)
        dqf[1, :, hs] = tn(ds, k)

    def pa_copy(i):
        return pltpu.make_async_remote_copy(
            src_ref=ps.at[pl.ds(lax.rem(ix + i, nx) * ny, ny)], dst_ref=pa.at[ix],
            send_sem=pa_ss.at[i], recv_sem=pa_rs.at[i], device_id=(ia, x_peer(i), it), device_id_type=MESH,
        )

    def pb_copy(i):
        return pltpu.make_async_remote_copy(
            src_ref=s1.at[lax.rem(iy + i, ny)], dst_ref=pb.at[iy],
            send_sem=pb_ss.at[i], recv_sem=pb_rs.at[i], device_id=(ia, y_peer(i), it), device_id_type=MESH,
        )

    def p2_copy(i):
        return pltpu.make_async_remote_copy(
            src_ref=u1.at[il], dst_ref=u1.at[il], send_sem=p2_ss.at[i],
            recv_sem=p2_rs.at[i], device_id=(l_peer(i), iw, it), device_id_type=MESH,
        )

    def p3_copy(i):
        return pltpu.make_async_remote_copy(
            src_ref=vz.at[iz], dst_ref=vz.at[iz], send_sem=p3_ss.at[i],
            recv_sem=p3_rs.at[i], device_id=(z_peer(i), iw, it), device_id_type=MESH,
        )

    def cy_copy(i):
        own_slot = ix * ny + iy
        return pltpu.make_async_remote_copy(
            src_ref=c4.at[own_slot], dst_ref=c4.at[own_slot],
            send_sem=cy_ss.at[i], recv_sem=cy_rs.at[i], device_id=(ia, y_peer(i), it), device_id_type=MESH,
        )

    def cw_copy(i):
        slots = pl.ds(ix * ny, ny)
        return pltpu.make_async_remote_copy(
            src_ref=c4.at[slots], dst_ref=c4.at[slots],
            send_sem=cw_ss.at[i], recv_sem=cw_rs.at[i], device_id=(ia, x_peer(i), it), device_id_type=MESH,
        )

    c3_copy = pltpu.make_async_remote_copy(
        src_ref=c3.at[0], dst_ref=c3.at[1], send_sem=c3_ss, recv_sem=c3_rs,
        device_id=(ia, iw, 1 - it), device_id_type=MESH,
    )

    for i in range(1, nx):
        pa_copy(i).start()

    loads[4].wait()
    cols = 2 * nw
    table = nb.shape[1]
    tiles = [(r - 1, c) for r in range(3) for c in (0, 1)] + [(r - 1, c) for r in range(3) for c in (-1, 2)]
    which = lax.broadcasted_iota(jnp.int32, (16, table), 0)
    numbers = jnp.full((16, table), -5, jnp.int32)
    for n, (r, c) in enumerate(tiles):
        row, col = ia + r, 2 * iw + c
        fine = (row >= 0) & (row < nh) & (col >= 0) & (col < cols)
        numbers = jnp.where(which == n, jnp.where(fine, row * cols + col, -5), numbers)
    chosen = jnp.where(lax.broadcasted_iota(jnp.int32, (16, table), 1) == numbers, 1.0, 0.0)
    lane = lax.broadcasted_iota(jnp.int32, (1, 128), 1)
    for side in range(2):
        hit = jnp.max(jnp.where(nb[...] == ia * cols + 2 * iw + side, 1.0, 0.0), axis=0, keepdims=True)
        hit = jnp.broadcast_to(jnp.max(chosen * hit, axis=1, keepdims=True), (16, 128))
        for b in range(6):
            pen[b, side:side + 1, :] = BIG * (1.0 - jnp.where(lane < 64, hit[2 * b:2 * b + 1], hit[2 * b + 1:2 * b + 2]))

    loads[6].wait()

    def attend(b, c=None, first=False):
        for h in range(heads) if c is None else range(per_chunk * c, per_chunk * (c + 1)):
            hs = slice(HD * h, HD * h + HD)
            k, v, q, g = kv[0, :, hs], kv[1, :, hs], qg[b, 0, :, hs], qg[b, 1, :, hs]
            total = (lro[b, h:h + 1, :] + pen[b, 0:2, :]).reshape(1, 2, 1, 128)
            p = jnp.exp(nt(k, q).reshape(TS, 2, TS, 128) * factor - total).reshape(128, 128)
            ds = (factor * p * (nt(v, g) - lro[b, 8 + h:9 + h, :])).astype(BF16)
            dk, dv = nn(ds, q), nn(p.astype(BF16), g)
            if first:
                dkv_acc[0, :, hs] = dk
                dkv_acc[1, :, hs] = dv
                dqf[b, :, hs] += tn(ds, k)
            else:
                dkv_acc[0, :, hs] += dk
                dkv_acc[1, :, hs] += dv
                dqf[b, :, hs] = tn(ds, k)

    def totals_centre(n):
        lr_copy(n).wait_recv()
        lro[block_of(*STEPS[n])] = lrx[n]

    def totals_outer(west, east):
        lr_copy(west).wait_recv()
        lr_copy(east).wait_recv()
        both = jnp.where(lax.broadcasted_iota(jnp.int32, (16, 128), 1) < 64, lrx[east], lrx[west])
        lro[block_of(*STEPS[west])] = pltpu.roll(both, 64, 1)

    def beside_arrives(c):
        for s in SIDES:
            qg_copy(STEPS.index((0, s)), c).wait_recv()
            for e in SIDES:
                @pl.when(relay_z[e, s])
                def _():
                    forward_z(e, s, c).start()

    def above_below_arrive(c):
        for dr in SIDES:
            @pl.when(has[dr])
            def _():
                qg_copy(STEPS.index((dr, 0)), c).wait_recv()
            for t in SIDES:
                @pl.when(relay_x[dr, t])
                def _():
                    forward_x(dr, t, c).start()

    def send_beside(c, s):
        dq_send[4, rows_of(s), lanes(c)] = dqf[4, rows_of(s), lanes(c)].astype(BF16)
        dq_copy(STEPS.index((0, s)), c).start()

    def attend_beside(c):
        attend(4, c)
        for s in SIDES:
            @pl.when(jnp.logical_not(at_seam[s]))
            def _():
                send_beside(c, s)

    def attend_corners(c):
        for dr in SIDES:
            b = block_of(dr, 1)
            for s in SIDES:
                @pl.when(has[dr])
                def _():
                    qg_copy(STEPS.index((dr, s)), c).wait_recv()
            attend(b, c)
            dq_send[b, :, lanes(c)] = dqf[b, :, lanes(c)].astype(BF16)
            for s in SIDES:
                @pl.when(mine_x[dr, s])
                def _():
                    corner_x(dr, s, c).start()

                @pl.when(mine_z[dr, s])
                def _():
                    corner_z(dr, s, c).start()

                if (dr, s) in diagonal:
                    @pl.when(mine_s[dr, s])
                    def _():
                        dq_copy(STEPS.index((dr, s)), c).start()

    def fold(c):
        for s in SIDES:
            for e in SIDES:
                @pl.when(relay_z[e, s])
                def _():
                    corner_z(-e, s, c).wait_recv()
                    dqf[4, rows_of(s), lanes(c)] += cz[bit(e), bit(s), :, lanes(c)].astype(F32)

            @pl.when(at_seam[s])
            def _():
                send_beside(c, s)
        for dr in SIDES:
            for t in SIDES:
                @pl.when(relay_x[dr, t])
                def _():
                    corner_x(dr, -t, c).wait_recv()
                    dqf[dr + 1, rows_of(t), lanes(c)] += cx[bit(dr), bit(t), :, lanes(c)].astype(F32)
            dq_send[dr + 1, :, lanes(c)] = dqf[dr + 1, :, lanes(c)].astype(BF16)

            @pl.when(has[dr])
            def _():
                dq_copy(STEPS.index((dr, 0)), c).start()

    def sum_over_x():
        for i in range(1, nx):
            pa_copy(i).wait_recv()
        pa[ix] = ps[pl.ds(ix * ny, ny)]
        for j in range(ny):
            acc = pa[0, j].astype(F32)
            for i in range(1, nx):
                acc = acc + pa[i, j].astype(F32)
            s1[j] = acc
        for i in range(1, ny):
            pb_copy(i).start()

    def sum_over_y():
        for i in range(1, ny):
            pb_copy(i).wait_recv()
        pb[iy] = s1[iy]
        acc = pb[0]
        for j in range(1, ny):
            acc = acc + pb[j]
        u1[il] = acc
        for i in range(1, nl):
            p2_copy(i).start()

    def sum_over_rows():
        for i in range(1, nl):
            p2_copy(i).wait_recv()
        acc = u1[0]
        for j in range(1, nl):
            acc = acc + u1[j]
        vz[iz] = acc.astype(BF16)
        for i in range(1, nz):
            p3_copy(i).start()

    def project():
        for i in range(1, nz):
            p3_copy(i).wait_recv()
        loads[7].wait()
        acc = vz[0].astype(F32)
        for j in range(1, nz):
            acc = acc + vz[j].astype(F32)
        acc = acc.astype(BF16)
        c3[0] = nt(acc[:tr], proj[0]) + nt(acc[tr:], proj[1])
        c3_copy.start()

    def gather_over_y():
        c3_copy.wait_recv()
        c4[ix * ny + iy] = c3[0] + c3[1]
        for i in range(1, ny):
            cy_copy(i).start()

    def gather_over_x():
        for i in range(1, ny):
            cy_copy(i).wait_recv()
        for i in range(1, nx):
            cw_copy(i).start()

    def write_context():
        for i in range(1, nx):
            cw_copy(i).wait_recv()
        ctx_out[...] = c4[...].reshape(nw * tr, c4.shape[2]).T

    def write_keys():
        for n in range(2):
            for i in range(4):
                dkv_out[n, 32 * i:32 * i + 32, :] = dkv_acc[n, 32 * i:32 * i + 32, :].astype(BF16)

    def write_queries():
        for c in range(CHUNKS):
            for s in SIDES:
                dq_copy(STEPS.index((0, s)), c).wait_recv()
            for dr in SIDES:
                @pl.when(has[-dr])
                def _():
                    dq_copy(STEPS.index((dr, 0)), c).wait_recv()
            for a, b in diagonal:
                @pl.when(to_s[a, b])
                def _():
                    dq_copy(STEPS.index((-a, -b)), c).wait_recv()
                    dqf[1, rows_of(b), lanes(c)] += dq_recv[block_of(a, b), rows_of(b), lanes(c)].astype(F32)
        for i in range(4):
            sums = []
            for start in (16 * i, 64 + 16 * i):
                rows = slice(start, start + 16)
                x = dqf[1, rows, :]
                for b in (0, 2, 4):
                    x = x + dq_recv[b, rows, :].astype(F32)
                sums.append(x)
            a, b = sums
            dq_out[32 * i:32 * i + 32, :] = jnp.concatenate([a[0:8], b[0:8], a[8:16], b[8:16]], 0).astype(BF16)

    attend(1, first=True)
    for dr in SIDES:
        @pl.when(relays[dr])
        def _():
            hop_copy(dr).wait_recv()
            hop_forward(dr).start()
    totals_outer(2, 3)
    beside_arrives(0)
    sum_over_x()
    for c in range(1, CHUNKS):
        beside_arrives(c)
    totals_centre(0)
    totals_centre(1)
    above_below_arrive(0)
    attend_beside(0)
    sum_over_y()
    for c in range(1, CHUNKS):
        above_below_arrive(c)
    for c in range(1, CHUNKS):
        attend_beside(c)
    attend(0, 0)
    attend(2, 0)
    sum_over_rows()
    for c in range(1, CHUNKS):
        attend(0, c)
        attend(2, c)
    totals_outer(4, 5)
    totals_outer(6, 7)
    attend_corners(0)
    project()
    for c in range(1, CHUNKS):
        attend_corners(c)
    gather_over_y()
    for c in range(CHUNKS):
        fold(c)
    write_keys()
    gather_over_x()
    write_queries()
    write_context()

    for c in range(CHUNKS):
        for s in SIDES:
            qg_copy(STEPS.index((0, s)), c).wait_send()
            dq_copy(STEPS.index((0, s)), c).wait_send()

            @pl.when(passes[s] if c == CHUNKS - 1 else has[-s])
            def _():
                qg_copy(STEPS.index((s, 0)), c).wait_send()

            @pl.when(has[s])
            def _():
                dq_copy(STEPS.index((s, 0)), c).wait_send()
        for a, b in diagonal:
            @pl.when(to_s[a, b])
            def _():
                qg_copy(STEPS.index((-a, -b)), c).wait_send()

            @pl.when(mine_s[a, b])
            def _():
                dq_copy(STEPS.index((a, b)), c).wait_send()
        for a, b in pairs:
            @pl.when(both(has[a], jnp.logical_not(mine_s[a, b])))
            def _():
                corner_x(a, b, c).wait_send()

            @pl.when(relay_x[a, b])
            def _():
                forward_x(a, b, c).wait_send()

            @pl.when(relay_z[a, b])
            def _():
                forward_z(a, b, c).wait_send()
    for dr in SIDES:
        @pl.when(hops[dr])
        def _():
            hop_copy(dr).wait_send()

        @pl.when(relays[dr])
        def _():
            hop_forward(dr).wait_send()
    for n in range(8):
        lr_copy(n).wait_send()
    for i in range(1, nx):
        pa_copy(i).wait_send()
        cw_copy(i).wait_send()
    for i in range(1, ny):
        pb_copy(i).wait_send()
        cy_copy(i).wait_send()
    c3_copy.wait_send()
    for i in range(1, nl):
        p2_copy(i).wait_send()
    for i in range(1, nz):
        p3_copy(i).wait_send()


def solution(mesh):
    nh, nw = mesh.shape["ha"], mesh.shape["wa"]
    nx = min(RING_X, nw)
    ny = nw // nx
    nz = min(RING_Z, nh)
    nl = nh // nz

    def local(queries, keys_values, grad_out, log_totals, row_deltas, prompt_kv, prompt_proj, neighbours, prompt_length):
        rows_here, cols_here, width = queries.shape
        heads = log_totals.shape[-1]
        cells = rows_here * cols_here
        text = prompt_kv.shape[1]
        outs = prompt_proj.shape[1]
        tr = text // nw
        any_space = pl.BlockSpec(memory_space=pl.ANY)
        vmem = pl.BlockSpec(memory_space=pltpu.VMEM)
        dma = pltpu.SemaphoreType.DMA
        two = lambda n: [dma((n,)), dma((n,))]
        dq, dkv, ctx = pl.pallas_call(
            functools.partial(kernel, nh, nw, heads),
            out_shape=(
                jax.ShapeDtypeStruct((cells, width), BF16),
                jax.ShapeDtypeStruct((2, cells, width), BF16),
                jax.ShapeDtypeStruct((outs, text), F32),
            ),
            in_specs=[any_space] * 8 + [pl.BlockSpec(memory_space=pltpu.SMEM)],
            out_specs=(vmem, vmem, vmem),
            scratch_shapes=[
                pltpu.VMEM((cells, width), BF16),
                pltpu.VMEM((2, cells, width), BF16),
                pltpu.VMEM((cells, width), BF16),
                pltpu.VMEM((heads, rows_here, cols_here), F32),
                pltpu.VMEM((heads, rows_here, cols_here), F32),
                pltpu.VMEM((2, text, width), BF16),
                pltpu.VMEM((2, outs, width), BF16),
                pltpu.VMEM(neighbours.shape[::-1], jnp.int32),
                pltpu.VMEM((6, 2, cells, width), BF16),
                pltpu.VMEM((2, 2, cells, width // CHUNKS), BF16),
                pltpu.VMEM((8, 16, cells), F32),
                pltpu.VMEM((6, 16, cells), F32),
                pltpu.VMEM((6, 8, cells), F32),
                pltpu.VMEM((6, cells, width), F32),
                pltpu.VMEM((6, cells, width), BF16),
                pltpu.VMEM((6, cells, width), BF16),
                pltpu.VMEM((2, 2, CELLS, width), BF16),
                pltpu.VMEM((2, 2, CELLS, width), BF16),
                pltpu.VMEM((2, cells, width), F32),
                pltpu.VMEM((nw, 2 * tr, width), BF16),
                pltpu.VMEM((nx, ny, 2 * tr, width), BF16),
                pltpu.VMEM((ny, 2 * tr, width), F32),
                pltpu.VMEM((ny, 2 * tr, width), F32),
                pltpu.VMEM((nl, 2 * tr, width), F32),
                pltpu.VMEM((nz, 2 * tr, width), BF16),
                pltpu.VMEM((2, tr, outs), F32),
                pltpu.VMEM((nw, tr, outs), F32),
                dma((8,)),
                dma((CHUNKS, 8)), dma((CHUNKS, 8)), dma((CHUNKS, 8)), dma((2,)), *two(2), *two(8),
                dma((CHUNKS, 8)), dma((CHUNKS, 8)), dma((CHUNKS, 4)), dma((CHUNKS, 4)), dma((CHUNKS, 4)),
                *two(nx), *two(ny), *two(nl), *two(nz), dma, dma, *two(ny), *two(nx),
            ],
            compiler_params=pltpu.CompilerParams(
                collective_id=0, has_side_effects=True, vmem_limit_bytes=63 * 2**20
            ),
            name="tile_attention_grads",
        )(
            queries.reshape(cells, width), keys_values.reshape(2, cells, width), grad_out.reshape(cells, width),
            jnp.transpose(log_totals, (2, 0, 1)), jnp.transpose(row_deltas, (2, 0, 1)),
            prompt_kv, prompt_proj, neighbours.T, prompt_length,
        )
        return (
            dq.reshape(rows_here, cols_here, width),
            dkv.reshape(2, rows_here, cols_here, width),
            ctx.T,
        )

    placed = P("ha", "wa", "ta")
    return jax.shard_map(
        local,
        mesh=mesh,
        in_specs=(placed, P(None, "ha", "wa", "ta"), placed, placed, placed, P(None, None, "ta"), P(None, "ha", "ta"), P(), P()),
        out_specs=(placed, P(None, "ha", "wa", "ta"), P(None, "ha")),
        check_vma=False,
    )
```

```python
import functools

import jax
import jax.numpy as jnp
from jax import lax
from jax.experimental import pallas as pl
from jax.experimental.pallas import tpu as pltpu
from jax.sharding import PartitionSpec as P

MESH = pl.DeviceIdType.MESH
F32 = jnp.float32
BF16 = jnp.bfloat16
TS = 8
CELLS = TS * TS
HD = 128
BIG = 1e30
RING_X = 4
RING_Z = 8
CHUNKS = 2
STEPS = [(-1, 0), (1, 0), (0, -1), (0, 1), (-1, -1), (-1, 1), (1, -1), (1, 1)]
SIDES = (-1, 1)


def block_of(row_step, col_step):
    return row_step + 1 if col_step == 0 else row_step + 4


def rows_of(col_step):
    return {0: slice(0, 128), -1: slice(0, 64), 1: slice(64, 128)}[col_step]


def bit(step):
    return (step + 1) // 2


def nt(a, b):
    return lax.dot_general(a, b, (((1,), (1,)), ((), ())), preferred_element_type=F32)


def nn(a, b):
    return lax.dot_general(a, b, (((1,), (0,)), ((), ())), preferred_element_type=F32)


def tn(a, b):
    return lax.dot_general(a, b, (((0,), (0,)), ((), ())), preferred_element_type=F32)


def kernel(
    nh, nw, heads,
    q_hbm, kv_hbm, g_hbm, lt_hbm, rd_hbm, pkv_hbm, proj_hbm, nb_hbm, plen_ref,
    dq_out, dkv_out, ctx_out,
    qn, kv, gn, ltn, rdn, pkv, proj, nb,
    qg, held, lrx, lro, pen, dqf, dq_send, dq_recv, cx, cz, dkv_acc,
    ps, pa, s1, pb, u1, vz, c3, c4,
    ld_sem, qg_ss, qg_rs, fw_ss, hp_ss, hp_rs, hf_ss, lr_ss, lr_rs, dq_ss, dq_rs, co_ss, cx_rs, cz_rs,
    pa_ss, pa_rs, pb_ss, pb_rs, p2_ss, p2_rs, p3_ss, p3_rs, c3_ss, c3_rs, cy_ss, cy_rs, cw_ss, cw_rs,
):
    width = heads * HD
    nx = min(RING_X, nw)
    ny = nw // nx
    ia, iw, it = lax.axis_index("ha"), lax.axis_index("wa"), lax.axis_index("ta")
    ix, iy = lax.rem(iw, nx), iw // nx
    nz = min(RING_Z, nh)
    nl = nh // nz
    iz, il = lax.rem(ia, nz), ia // nz
    factor = HD ** -0.5
    tr = 128 // nw
    per_chunk = heads // CHUNKS

    def place(row_step, col_step):
        return lax.rem(ia + row_step + nh, nh), lax.rem(iw + col_step + nw, nw)

    def at(row_step, col_step):
        return place(row_step, col_step) + (it,)

    def seam(column, side):
        return lax.rem(column, RING_X) == (0 if side < 0 else RING_X - 1)

    def there(row_step):
        return ia > 0 if row_step < 0 else ia < nh - 1

    def by_x(who, row_step, side):
        return jnp.logical_not(seam(who[1], side))

    def straight(who, row_step, side):
        if row_step == side:
            return ia < 0
        across = lax.rem(who[0], RING_Z) == (0 if row_step < 0 else RING_Z - 1)
        return jnp.logical_and(seam(who[1], side), across)

    def by_z(who, row_step, side):
        return jnp.logical_and(seam(who[1], side), jnp.logical_not(straight(who, row_step, side)))

    def both(a, b):
        return jnp.logical_and(a, b)

    def lanes(c):
        return slice(HD * per_chunk * c, HD * per_chunk * (c + 1))

    barrier = pltpu.get_barrier_semaphore()

    def greet(who):
        pl.semaphore_signal(barrier, inc=1, device_id=who, device_id_type=MESH)

    def x_peer(i):
        return iy * nx + lax.rem(ix + i, nx)

    def y_peer(i):
        return lax.rem(iy + i, ny) * nx + ix

    def l_peer(i):
        return lax.rem(il + i, nl) * nz + iz

    def z_peer(i):
        return il * nz + lax.rem(iz + i, nz)

    for step in STEPS:
        greet(at(*step))
    for i in range(1, nx):
        greet((ia, x_peer(i), it))
    for i in range(1, ny):
        greet((ia, y_peer(i), it))
    for i in range(1, nl):
        greet((l_peer(i), iw, it))
    for i in range(1, nz):
        greet((z_peer(i), iw, it))
    greet((ia, iw, 1 - it))

    loads = [
        pltpu.make_async_copy(src, dst, ld_sem.at[n])
        for n, (src, dst) in enumerate(
            [(q_hbm, qn), (g_hbm, gn), (lt_hbm, ltn), (rd_hbm, rdn), (nb_hbm, nb),
             (pkv_hbm, pkv), (kv_hbm, kv), (proj_hbm, proj)]
        )
    ]
    for load in loads:
        load.start()

    for n, source in ((0, qn), (1, gn)):
        loads[n].wait()
        for i in range(4):
            x = source[32 * i:32 * i + 32, :].astype(F32)
            qg[1, n, 16 * i:16 * i + 16, :] = jnp.concatenate([x[0:8], x[16:24]], 0).astype(BF16)
            qg[1, n, 64 + 16 * i:80 + 16 * i, :] = jnp.concatenate([x[8:16], x[24:32]], 0).astype(BF16)
    for n, source in ((0, ltn), (1, rdn)):
        loads[2 + n].wait()
        pieces = [source[:, r, TS * s:TS * s + TS] for s in (0, 1) for r in range(TS)]
        lro[1, 8 * n:8 * n + heads, :] = jnp.concatenate(pieces, 1)

    pl.semaphore_wait(barrier, 8 + (nx - 1) + (ny - 1) + (nl - 1) + (nz - 1) + 1)

    def qg_copy(n, c):
        dr, dc = STEPS[n]
        return pltpu.make_async_remote_copy(
            src_ref=qg.at[1, :, rows_of(-dc), lanes(c)],
            dst_ref=qg.at[block_of(dr, dc), :, rows_of(dc), lanes(c)],
            send_sem=qg_ss.at[c, n], recv_sem=qg_rs.at[c, n],
            device_id=at(-dr, -dc), device_id_type=MESH,
        )

    def forward_x(dr, t, c):
        return pltpu.make_async_remote_copy(
            src_ref=qg.at[block_of(dr, 0), :, rows_of(t), lanes(c)],
            dst_ref=qg.at[block_of(dr, -t), :, rows_of(-t), lanes(c)],
            send_sem=fw_ss.at[c, 2 * bit(dr) + bit(t)], recv_sem=qg_rs.at[c, STEPS.index((dr, -t))],
            device_id=at(0, t), device_id_type=MESH,
        )

    def forward_z(e, s, c):
        return pltpu.make_async_remote_copy(
            src_ref=qg.at[block_of(0, s), :, rows_of(s), lanes(c)],
            dst_ref=qg.at[block_of(-e, s), :, rows_of(s), lanes(c)],
            send_sem=fw_ss.at[c, 4 + 2 * bit(e) + bit(s)], recv_sem=qg_rs.at[c, STEPS.index((-e, s))],
            device_id=at(e, 0), device_id_type=MESH,
        )

    def hop_copy(dr):
        return pltpu.make_async_remote_copy(
            src_ref=qg.at[1, :, :, lanes(CHUNKS - 1)], dst_ref=held.at[bit(dr)],
            send_sem=hp_ss.at[bit(dr)], recv_sem=hp_rs.at[bit(dr)],
            device_id=(il * nz + lax.rem(iz - dr + nz, nz), iw, it), device_id_type=MESH,
        )

    def hop_forward(dr):
        return pltpu.make_async_remote_copy(
            src_ref=held.at[bit(dr)], dst_ref=qg.at[block_of(dr, 0), :, :, lanes(CHUNKS - 1)],
            send_sem=hf_ss.at[bit(dr)], recv_sem=qg_rs.at[CHUNKS - 1, STEPS.index((dr, 0))],
            device_id=(lax.rem(ia - dr * nz + nh, nh), iw, it), device_id_type=MESH,
        )

    def lr_copy(n):
        dr, dc = STEPS[n]
        return pltpu.make_async_remote_copy(
            src_ref=lro.at[1], dst_ref=lrx.at[n],
            send_sem=lr_ss.at[n], recv_sem=lr_rs.at[n],
            device_id=at(-dr, -dc), device_id_type=MESH,
        )

    def dq_copy(n, c):
        dr, dc = STEPS[n]
        return pltpu.make_async_remote_copy(
            src_ref=dq_send.at[block_of(dr, dc), rows_of(dc), lanes(c)],
            dst_ref=dq_recv.at[block_of(-dr, -dc), rows_of(-dc), lanes(c)],
            send_sem=dq_ss.at[c, n], recv_sem=dq_rs.at[c, n],
            device_id=at(dr, dc), device_id_type=MESH,
        )

    def corner_x(dr, s, c):
        return pltpu.make_async_remote_copy(
            src_ref=dq_send.at[block_of(dr, s), rows_of(s), lanes(c)],
            dst_ref=cx.at[bit(dr), bit(-s), :, lanes(c)],
            send_sem=co_ss.at[c, 2 * bit(dr) + bit(s)], recv_sem=cx_rs.at[c, 2 * bit(dr) + bit(-s)],
            device_id=at(0, s), device_id_type=MESH,
        )

    def corner_z(dr, s, c):
        return pltpu.make_async_remote_copy(
            src_ref=dq_send.at[block_of(dr, s), rows_of(s), lanes(c)],
            dst_ref=cz.at[bit(-dr), bit(s), :, lanes(c)],
            send_sem=co_ss.at[c, 2 * bit(dr) + bit(s)], recv_sem=cz_rs.at[c, 2 * bit(-dr) + bit(s)],
            device_id=at(dr, 0), device_id_type=MESH,
        )

    pairs = [(a, b) for a in SIDES for b in SIDES]
    has = {dr: there(dr) for dr in SIDES}
    mine_x = {(dr, s): both(has[dr], by_x((ia, iw), dr, s)) for dr, s in pairs}
    mine_z = {(dr, s): both(has[dr], by_z((ia, iw), dr, s)) for dr, s in pairs}
    mine_s = {(dr, s): both(has[dr], straight((ia, iw), dr, s)) for dr, s in pairs}
    relay_x = {(dr, t): both(has[dr], by_x(place(0, t), dr, -t)) for dr, t in pairs}
    relay_z = {(e, s): both(has[e], by_z(place(e, 0), -e, s)) for e, s in pairs}
    to_s = {(a, b): both(has[a], straight(place(a, b), -a, -b)) for a, b in pairs}
    at_seam = {s: seam(iw, s) for s in SIDES}
    crowded = {-1: ix == nx - 1, 1: ix == 0}
    hops = {
        -1: both(crowded[-1], both(iz == nz - 1, has[1])),
        1: both(crowded[1], both(iz == 0, has[-1])),
    }
    relays = {
        -1: both(crowded[-1], both(iz == 0, ia + nz < nh)),
        1: both(crowded[1], both(iz == nz - 1, ia >= nz)),
    }
    passes = {dr: both(has[-dr], jnp.logical_not(hops[dr])) for dr in SIDES}
    diagonal = [(a, b) for a, b in pairs if a != b]

    for n in range(8):
        lr_copy(n).start()
    for c in range(CHUNKS):
        for s in SIDES:
            qg_copy(STEPS.index((0, s)), c).start()
        for dr in SIDES:
            @pl.when(passes[dr] if c == CHUNKS - 1 else has[-dr])
            def _():
                qg_copy(STEPS.index((dr, 0)), c).start()

            if c == CHUNKS - 1:
                @pl.when(hops[dr])
                def _():
                    hop_copy(dr).start()
        for a, b in diagonal:
            @pl.when(to_s[a, b])
            def _():
                qg_copy(STEPS.index((-a, -b)), c).start()
    for dr in SIDES:
        @pl.when(jnp.logical_not(has[dr]))
        def _():
            qg[dr + 1] = jnp.zeros(qg.shape[1:], BF16)
            qg[dr + 4] = jnp.zeros(qg.shape[1:], BF16)
            dq_recv[dr + 1] = jnp.zeros(dq_recv.shape[1:], BF16)
    loads[5].wait()
    live = lax.broadcasted_iota(jnp.int32, (128, 128), 0) < plen_ref[0]
    for h in range(heads):
        hs = slice(HD * h, HD * h + HD)
        k, v, q, g = pkv[0, :, hs], pkv[1, :, hs], qg[1, 0, :, hs], qg[1, 1, :, hs]
        p = jnp.exp(jnp.where(live, nt(k, q) * factor - lro[1, h:h + 1, :], -BIG))
        ds = (factor * p * (nt(v, g) - lro[1, 8 + h:9 + h, :])).astype(BF16)
        dk = nn(ds, q).reshape(nw, tr, HD)
        dv = nn(p.astype(BF16), g).reshape(nw, tr, HD)
        ps[:, :, hs] = jnp.concatenate([dk, dv], 1).astype(BF16)
        dqf[1, :, hs] = tn(ds, k)

    def pa_copy(i):
        return pltpu.make_async_remote_copy(
            src_ref=ps.at[pl.ds(lax.rem(ix + i, nx) * ny, ny)], dst_ref=pa.at[ix],
            send_sem=pa_ss.at[i], recv_sem=pa_rs.at[i], device_id=(ia, x_peer(i), it), device_id_type=MESH,
        )

    def pb_copy(i):
        return pltpu.make_async_remote_copy(
            src_ref=s1.at[lax.rem(iy + i, ny)], dst_ref=pb.at[iy],
            send_sem=pb_ss.at[i], recv_sem=pb_rs.at[i], device_id=(ia, y_peer(i), it), device_id_type=MESH,
        )

    def p2_copy(i):
        return pltpu.make_async_remote_copy(
            src_ref=u1.at[il], dst_ref=u1.at[il], send_sem=p2_ss.at[i],
            recv_sem=p2_rs.at[i], device_id=(l_peer(i), iw, it), device_id_type=MESH,
        )

    def p3_copy(i):
        return pltpu.make_async_remote_copy(
            src_ref=vz.at[iz], dst_ref=vz.at[iz], send_sem=p3_ss.at[i],
            recv_sem=p3_rs.at[i], device_id=(z_peer(i), iw, it), device_id_type=MESH,
        )

    def cy_copy(i):
        own_slot = ix * ny + iy
        return pltpu.make_async_remote_copy(
            src_ref=c4.at[own_slot], dst_ref=c4.at[own_slot],
            send_sem=cy_ss.at[i], recv_sem=cy_rs.at[i], device_id=(ia, y_peer(i), it), device_id_type=MESH,
        )

    def cw_copy(i):
        slots = pl.ds(ix * ny, ny)
        return pltpu.make_async_remote_copy(
            src_ref=c4.at[slots], dst_ref=c4.at[slots],
            send_sem=cw_ss.at[i], recv_sem=cw_rs.at[i], device_id=(ia, x_peer(i), it), device_id_type=MESH,
        )

    c3_copy = pltpu.make_async_remote_copy(
        src_ref=c3.at[0], dst_ref=c3.at[1], send_sem=c3_ss, recv_sem=c3_rs,
        device_id=(ia, iw, 1 - it), device_id_type=MESH,
    )

    for i in range(1, nx):
        pa_copy(i).start()

    loads[4].wait()
    cols = 2 * nw
    table = nb.shape[1]
    tiles = [(r - 1, c) for r in range(3) for c in (0, 1)] + [(r - 1, c) for r in range(3) for c in (-1, 2)]
    which = lax.broadcasted_iota(jnp.int32, (16, table), 0)
    numbers = jnp.full((16, table), -5, jnp.int32)
    for n, (r, c) in enumerate(tiles):
        row, col = ia + r, 2 * iw + c
        fine = (row >= 0) & (row < nh) & (col >= 0) & (col < cols)
        numbers = jnp.where(which == n, jnp.where(fine, row * cols + col, -5), numbers)
    chosen = jnp.where(lax.broadcasted_iota(jnp.int32, (16, table), 1) == numbers, 1.0, 0.0)
    lane = lax.broadcasted_iota(jnp.int32, (1, 128), 1)
    for side in range(2):
        hit = jnp.max(jnp.where(nb[...] == ia * cols + 2 * iw + side, 1.0, 0.0), axis=0, keepdims=True)
        hit = jnp.broadcast_to(jnp.max(chosen * hit, axis=1, keepdims=True), (16, 128))
        for b in range(6):
            pen[b, side:side + 1, :] = BIG * (1.0 - jnp.where(lane < 64, hit[2 * b:2 * b + 1], hit[2 * b + 1:2 * b + 2]))

    loads[6].wait()

    def attend(b, c=None, first=False):
        for h in range(heads) if c is None else range(per_chunk * c, per_chunk * (c + 1)):
            hs = slice(HD * h, HD * h + HD)
            k, v, q, g = kv[0, :, hs], kv[1, :, hs], qg[b, 0, :, hs], qg[b, 1, :, hs]
            total = (lro[b, h:h + 1, :] + pen[b, 0:2, :]).reshape(1, 2, 1, 128)
            p = jnp.exp(nt(k, q).reshape(TS, 2, TS, 128) * factor - total).reshape(128, 128)
            ds = (factor * p * (nt(v, g) - lro[b, 8 + h:9 + h, :])).astype(BF16)
            dk, dv = nn(ds, q), nn(p.astype(BF16), g)
            if first:
                dkv_acc[0, :, hs] = dk
                dkv_acc[1, :, hs] = dv
                dqf[b, :, hs] += tn(ds, k)
            else:
                dkv_acc[0, :, hs] += dk
                dkv_acc[1, :, hs] += dv
                dqf[b, :, hs] = tn(ds, k)

    def totals_centre(n):
        lr_copy(n).wait_recv()
        lro[block_of(*STEPS[n])] = lrx[n]

    def totals_outer(west, east):
        lr_copy(west).wait_recv()
        lr_copy(east).wait_recv()
        both = jnp.where(lax.broadcasted_iota(jnp.int32, (16, 128), 1) < 64, lrx[east], lrx[west])
        lro[block_of(*STEPS[west])] = pltpu.roll(both, 64, 1)

    def beside_arrives(c):
        for s in SIDES:
            qg_copy(STEPS.index((0, s)), c).wait_recv()
            for e in SIDES:
                @pl.when(relay_z[e, s])
                def _():
                    forward_z(e, s, c).start()

    def above_below_arrive(c):
        for dr in SIDES:
            @pl.when(has[dr])
            def _():
                qg_copy(STEPS.index((dr, 0)), c).wait_recv()
            for t in SIDES:
                @pl.when(relay_x[dr, t])
                def _():
                    forward_x(dr, t, c).start()

    def send_beside(c, s):
        dq_send[4, rows_of(s), lanes(c)] = dqf[4, rows_of(s), lanes(c)].astype(BF16)
        dq_copy(STEPS.index((0, s)), c).start()

    def attend_beside(c):
        attend(4, c)
        for s in SIDES:
            @pl.when(jnp.logical_not(at_seam[s]))
            def _():
                send_beside(c, s)

    def attend_corners(c):
        for dr in SIDES:
            b = block_of(dr, 1)
            for s in SIDES:
                @pl.when(has[dr])
                def _():
                    qg_copy(STEPS.index((dr, s)), c).wait_recv()
            attend(b, c)
            dq_send[b, :, lanes(c)] = dqf[b, :, lanes(c)].astype(BF16)
            for s in SIDES:
                @pl.when(mine_x[dr, s])
                def _():
                    corner_x(dr, s, c).start()

                @pl.when(mine_z[dr, s])
                def _():
                    corner_z(dr, s, c).start()

                if (dr, s) in diagonal:
                    @pl.when(mine_s[dr, s])
                    def _():
                        dq_copy(STEPS.index((dr, s)), c).start()

    def fold(c):
        for s in SIDES:
            for e in SIDES:
                @pl.when(relay_z[e, s])
                def _():
                    corner_z(-e, s, c).wait_recv()
                    dqf[4, rows_of(s), lanes(c)] += cz[bit(e), bit(s), :, lanes(c)].astype(F32)

            @pl.when(at_seam[s])
            def _():
                send_beside(c, s)
        for dr in SIDES:
            for t in SIDES:
                @pl.when(relay_x[dr, t])
                def _():
                    corner_x(dr, -t, c).wait_recv()
                    dqf[dr + 1, rows_of(t), lanes(c)] += cx[bit(dr), bit(t), :, lanes(c)].astype(F32)
            dq_send[dr + 1, :, lanes(c)] = dqf[dr + 1, :, lanes(c)].astype(BF16)

            @pl.when(has[dr])
            def _():
                dq_copy(STEPS.index((dr, 0)), c).start()

    def sum_over_x():
        for i in range(1, nx):
            pa_copy(i).wait_recv()
        pa[ix] = ps[pl.ds(ix * ny, ny)]
        for j in range(ny):
            acc = pa[0, j].astype(F32)
            for i in range(1, nx):
                acc = acc + pa[i, j].astype(F32)
            s1[j] = acc
        for i in range(1, ny):
            pb_copy(i).start()

    def sum_over_y():
        for i in range(1, ny):
            pb_copy(i).wait_recv()
        pb[iy] = s1[iy]
        acc = pb[0]
        for j in range(1, ny):
            acc = acc + pb[j]
        u1[il] = acc
        for i in range(1, nl):
            p2_copy(i).start()

    def sum_over_rows():
        for i in range(1, nl):
            p2_copy(i).wait_recv()
        acc = u1[0]
        for j in range(1, nl):
            acc = acc + u1[j]
        vz[iz] = acc.astype(BF16)
        for i in range(1, nz):
            p3_copy(i).start()

    def project():
        for i in range(1, nz):
            p3_copy(i).wait_recv()
        loads[7].wait()
        acc = vz[0].astype(F32)
        for j in range(1, nz):
            acc = acc + vz[j].astype(F32)
        acc = acc.astype(BF16)
        c3[0] = nt(acc[:tr], proj[0]) + nt(acc[tr:], proj[1])
        c3_copy.start()

    def gather_over_y():
        c3_copy.wait_recv()
        c4[ix * ny + iy] = c3[0] + c3[1]
        for i in range(1, ny):
            cy_copy(i).start()

    def gather_over_x():
        for i in range(1, ny):
            cy_copy(i).wait_recv()
        for i in range(1, nx):
            cw_copy(i).start()

    def write_context():
        for i in range(1, nx):
            cw_copy(i).wait_recv()
        ctx_out[...] = c4[...].reshape(nw * tr, c4.shape[2]).T

    def write_keys():
        for n in range(2):
            for i in range(4):
                dkv_out[n, 32 * i:32 * i + 32, :] = dkv_acc[n, 32 * i:32 * i + 32, :].astype(BF16)

    def write_queries():
        for c in range(CHUNKS):
            for s in SIDES:
                dq_copy(STEPS.index((0, s)), c).wait_recv()
            for dr in SIDES:
                @pl.when(has[-dr])
                def _():
                    dq_copy(STEPS.index((dr, 0)), c).wait_recv()
            for a, b in diagonal:
                @pl.when(to_s[a, b])
                def _():
                    dq_copy(STEPS.index((-a, -b)), c).wait_recv()
                    dqf[1, rows_of(b), lanes(c)] += dq_recv[block_of(a, b), rows_of(b), lanes(c)].astype(F32)
        for i in range(4):
            sums = []
            for start in (16 * i, 64 + 16 * i):
                rows = slice(start, start + 16)
                x = dqf[1, rows, :]
                for b in (0, 2, 4):
                    x = x + dq_recv[b, rows, :].astype(F32)
                sums.append(x)
            a, b = sums
            dq_out[32 * i:32 * i + 32, :] = jnp.concatenate([a[0:8], b[0:8], a[8:16], b[8:16]], 0).astype(BF16)

    attend(1, first=True)
    for dr in SIDES:
        @pl.when(relays[dr])
        def _():
            hop_copy(dr).wait_recv()
            hop_forward(dr).start()
    totals_outer(2, 3)
    beside_arrives(0)
    sum_over_x()
    for c in range(1, CHUNKS):
        beside_arrives(c)
    totals_centre(0)
    totals_centre(1)
    above_below_arrive(0)
    attend_beside(0)
    sum_over_y()
    for c in range(1, CHUNKS):
        above_below_arrive(c)
    for c in range(1, CHUNKS):
        attend_beside(c)
    attend(0, 0)
    attend(2, 0)
    sum_over_rows()
    for c in range(1, CHUNKS):
        attend(0, c)
        attend(2, c)
    totals_outer(4, 5)
    totals_outer(6, 7)
    attend_corners(0)
    project()
    for c in range(1, CHUNKS):
        attend_corners(c)
    gather_over_y()
    write_keys()
    for c in range(CHUNKS):
        fold(c)
    gather_over_x()
    write_queries()
    write_context()

    for c in range(CHUNKS):
        for s in SIDES:
            qg_copy(STEPS.index((0, s)), c).wait_send()
            dq_copy(STEPS.index((0, s)), c).wait_send()

            @pl.when(passes[s] if c == CHUNKS - 1 else has[-s])
            def _():
                qg_copy(STEPS.index((s, 0)), c).wait_send()

            @pl.when(has[s])
            def _():
                dq_copy(STEPS.index((s, 0)), c).wait_send()
        for a, b in diagonal:
            @pl.when(to_s[a, b])
            def _():
                qg_copy(STEPS.index((-a, -b)), c).wait_send()

            @pl.when(mine_s[a, b])
            def _():
                dq_copy(STEPS.index((a, b)), c).wait_send()
        for a, b in pairs:
            @pl.when(both(has[a], jnp.logical_not(mine_s[a, b])))
            def _():
                corner_x(a, b, c).wait_send()

            @pl.when(relay_x[a, b])
            def _():
                forward_x(a, b, c).wait_send()

            @pl.when(relay_z[a, b])
            def _():
                forward_z(a, b, c).wait_send()
    for dr in SIDES:
        @pl.when(hops[dr])
        def _():
            hop_copy(dr).wait_send()

        @pl.when(relays[dr])
        def _():
            hop_forward(dr).wait_send()
    for n in range(8):
        lr_copy(n).wait_send()
    for i in range(1, nx):
        pa_copy(i).wait_send()
        cw_copy(i).wait_send()
    for i in range(1, ny):
        pb_copy(i).wait_send()
        cy_copy(i).wait_send()
    c3_copy.wait_send()
    for i in range(1, nl):
        p2_copy(i).wait_send()
    for i in range(1, nz):
        p3_copy(i).wait_send()


def deliver(a_in, b_in, c_in, a_out, b_out, c_out, a_mid, b_mid, c_mid, in_sem, out_sem):
    parts = [(b_in, b_mid, b_out), (a_in, a_mid, a_out), (c_in, c_mid, c_out)]
    reads = [pltpu.make_async_copy(src, mid, in_sem.at[n]) for n, (src, mid, _) in enumerate(parts)]
    writes = [pltpu.make_async_copy(mid, dst, out_sem.at[n]) for n, (_, mid, dst) in enumerate(parts)]
    for read in reads:
        read.start()
    for read, write in zip(reads, writes):
        read.wait()
        write.start()
    for write in writes:
        write.wait()


def solution(mesh):
    nh, nw = mesh.shape["ha"], mesh.shape["wa"]
    nx = min(RING_X, nw)
    ny = nw // nx
    nz = min(RING_Z, nh)
    nl = nh // nz

    def local(queries, keys_values, grad_out, log_totals, row_deltas, prompt_kv, prompt_proj, neighbours, prompt_length):
        rows_here, cols_here, width = queries.shape
        heads = log_totals.shape[-1]
        cells = rows_here * cols_here
        text = prompt_kv.shape[1]
        outs = prompt_proj.shape[1]
        tr = text // nw
        any_space = pl.BlockSpec(memory_space=pl.ANY)
        vmem = pl.BlockSpec(memory_space=pltpu.VMEM)
        dma = pltpu.SemaphoreType.DMA
        two = lambda n: [dma((n,)), dma((n,))]
        dq, dkv, ctx = pl.pallas_call(
            functools.partial(kernel, nh, nw, heads),
            out_shape=(
                jax.ShapeDtypeStruct((cells, width), BF16),
                jax.ShapeDtypeStruct((2, cells, width), BF16),
                jax.ShapeDtypeStruct((outs, text), F32),
            ),
            in_specs=[any_space] * 8 + [pl.BlockSpec(memory_space=pltpu.SMEM)],
            out_specs=(vmem, vmem, vmem),
            scratch_shapes=[
                pltpu.VMEM((cells, width), BF16),
                pltpu.VMEM((2, cells, width), BF16),
                pltpu.VMEM((cells, width), BF16),
                pltpu.VMEM((heads, rows_here, cols_here), F32),
                pltpu.VMEM((heads, rows_here, cols_here), F32),
                pltpu.VMEM((2, text, width), BF16),
                pltpu.VMEM((2, outs, width), BF16),
                pltpu.VMEM(neighbours.shape[::-1], jnp.int32),
                pltpu.VMEM((6, 2, cells, width), BF16),
                pltpu.VMEM((2, 2, cells, width // CHUNKS), BF16),
                pltpu.VMEM((8, 16, cells), F32),
                pltpu.VMEM((6, 16, cells), F32),
                pltpu.VMEM((6, 8, cells), F32),
                pltpu.VMEM((6, cells, width), F32),
                pltpu.VMEM((6, cells, width), BF16),
                pltpu.VMEM((6, cells, width), BF16),
                pltpu.VMEM((2, 2, CELLS, width), BF16),
                pltpu.VMEM((2, 2, CELLS, width), BF16),
                pltpu.VMEM((2, cells, width), F32),
                pltpu.VMEM((nw, 2 * tr, width), BF16),
                pltpu.VMEM((nx, ny, 2 * tr, width), BF16),
                pltpu.VMEM((ny, 2 * tr, width), F32),
                pltpu.VMEM((ny, 2 * tr, width), F32),
                pltpu.VMEM((nl, 2 * tr, width), F32),
                pltpu.VMEM((nz, 2 * tr, width), BF16),
                pltpu.VMEM((2, tr, outs), F32),
                pltpu.VMEM((nw, tr, outs), F32),
                dma((8,)),
                dma((CHUNKS, 8)), dma((CHUNKS, 8)), dma((CHUNKS, 8)), dma((2,)), *two(2), *two(8),
                dma((CHUNKS, 8)), dma((CHUNKS, 8)), dma((CHUNKS, 4)), dma((CHUNKS, 4)), dma((CHUNKS, 4)),
                *two(nx), *two(ny), *two(nl), *two(nz), dma, dma, *two(ny), *two(nx),
            ],
            compiler_params=pltpu.CompilerParams(
                collective_id=0, has_side_effects=True, vmem_limit_bytes=63 * 2**20
            ),
            name="tile_attention_grads",
        )(
            queries.reshape(cells, width), keys_values.reshape(2, cells, width), grad_out.reshape(cells, width),
            jnp.transpose(log_totals, (2, 0, 1)), jnp.transpose(row_deltas, (2, 0, 1)),
            prompt_kv, prompt_proj, neighbours.T, prompt_length,
        )
        results = (dq, dkv, ctx)
        dq, dkv, ctx = pl.pallas_call(
            deliver,
            out_shape=tuple(jax.ShapeDtypeStruct(x.shape, x.dtype) for x in results),
            in_specs=[any_space] * 3,
            out_specs=(any_space,) * 3,
            scratch_shapes=[pltpu.VMEM(x.shape, x.dtype) for x in results] + two(3),
            compiler_params=pltpu.CompilerParams(vmem_limit_bytes=62 * 2**20),
            name="deliver",
        )(*results)
        return (
            dq.reshape(rows_here, cols_here, width),
            dkv.reshape(2, rows_here, cols_here, width),
            ctx.T,
        )

    placed = P("ha", "wa", "ta")
    return jax.shard_map(
        local,
        mesh=mesh,
        in_specs=(placed, P(None, "ha", "wa", "ta"), placed, placed, placed, P(None, None, "ta"), P(None, "ha", "ta"), P(), P()),
        out_specs=(placed, P(None, "ha", "wa", "ta"), P(None, "ha")),
        check_vma=False,
    )
```

```python
import functools

import jax
import jax.numpy as jnp
from jax import lax
from jax.experimental import pallas as pl
from jax.experimental.pallas import tpu as pltpu
from jax.sharding import PartitionSpec as P

MESH = pl.DeviceIdType.MESH
F32 = jnp.float32
BF16 = jnp.bfloat16
TS = 8
CELLS = TS * TS
HD = 128
BIG = 1e30
RING_X = 4
RING_Z = 8
CHUNKS = 2
STEPS = [(-1, 0), (1, 0), (0, -1), (0, 1), (-1, -1), (-1, 1), (1, -1), (1, 1)]
SIDES = (-1, 1)


def block_of(row_step, col_step):
    return row_step + 1 if col_step == 0 else row_step + 4


def rows_of(col_step):
    return {0: slice(0, 128), -1: slice(0, 64), 1: slice(64, 128)}[col_step]


def bit(step):
    return (step + 1) // 2


def nt(a, b):
    return lax.dot_general(a, b, (((1,), (1,)), ((), ())), preferred_element_type=F32)


def nn(a, b):
    return lax.dot_general(a, b, (((1,), (0,)), ((), ())), preferred_element_type=F32)


def tn(a, b):
    return lax.dot_general(a, b, (((0,), (0,)), ((), ())), preferred_element_type=F32)


def kernel(
    nh, nw, heads,
    q_hbm, kv_hbm, g_hbm, lt_hbm, rd_hbm, pkv_hbm, proj_hbm, nb_hbm, plen_ref,
    dq_out, dkv_out, ctx_out,
    keys_low, key_sem, qn, kv, gn, ltn, rdn, pkv, proj, nb,
    qg, held, lrx, lro, pen, dqf, dq_send, dq_recv, cx, cz, dkv_acc,
    ps, pa, s1, pb, u1, vz, c3, c4,
    ld_sem, qg_ss, qg_rs, fw_ss, hp_ss, hp_rs, hf_ss, lr_ss, lr_rs, dq_ss, dq_rs, co_ss, cx_rs, cz_rs,
    pa_ss, pa_rs, pb_ss, pb_rs, p2_ss, p2_rs, p3_ss, p3_rs, c3_ss, c3_rs, cy_ss, cy_rs, cw_ss, cw_rs,
):
    width = heads * HD
    nx = min(RING_X, nw)
    ny = nw // nx
    ia, iw, it = lax.axis_index("ha"), lax.axis_index("wa"), lax.axis_index("ta")
    ix, iy = lax.rem(iw, nx), iw // nx
    nz = min(RING_Z, nh)
    nl = nh // nz
    iz, il = lax.rem(ia, nz), ia // nz
    factor = HD ** -0.5
    tr = 128 // nw
    per_chunk = heads // CHUNKS

    def place(row_step, col_step):
        return lax.rem(ia + row_step + nh, nh), lax.rem(iw + col_step + nw, nw)

    def at(row_step, col_step):
        return place(row_step, col_step) + (it,)

    def seam(column, side):
        return lax.rem(column, RING_X) == (0 if side < 0 else RING_X - 1)

    def there(row_step):
        return ia > 0 if row_step < 0 else ia < nh - 1

    def by_x(who, row_step, side):
        return jnp.logical_not(seam(who[1], side))

    def straight(who, row_step, side):
        if row_step == side:
            return ia < 0
        across = lax.rem(who[0], RING_Z) == (0 if row_step < 0 else RING_Z - 1)
        return jnp.logical_and(seam(who[1], side), across)

    def by_z(who, row_step, side):
        return jnp.logical_and(seam(who[1], side), jnp.logical_not(straight(who, row_step, side)))

    def both(a, b):
        return jnp.logical_and(a, b)

    def lanes(c):
        return slice(HD * per_chunk * c, HD * per_chunk * (c + 1))

    barrier = pltpu.get_barrier_semaphore()

    def greet(who):
        pl.semaphore_signal(barrier, inc=1, device_id=who, device_id_type=MESH)

    def x_peer(i):
        return iy * nx + lax.rem(ix + i, nx)

    def y_peer(i):
        return lax.rem(iy + i, ny) * nx + ix

    def l_peer(i):
        return lax.rem(il + i, nl) * nz + iz

    def z_peer(i):
        return il * nz + lax.rem(iz + i, nz)

    for step in STEPS:
        greet(at(*step))
    for i in range(1, nx):
        greet((ia, x_peer(i), it))
    for i in range(1, ny):
        greet((ia, y_peer(i), it))
    for i in range(1, nl):
        greet((l_peer(i), iw, it))
    for i in range(1, nz):
        greet((z_peer(i), iw, it))
    greet((ia, iw, 1 - it))

    loads = [
        pltpu.make_async_copy(src, dst, ld_sem.at[n])
        for n, (src, dst) in enumerate(
            [(q_hbm, qn), (g_hbm, gn), (lt_hbm, ltn), (rd_hbm, rdn), (nb_hbm, nb),
             (pkv_hbm, pkv), (kv_hbm, kv), (proj_hbm, proj)]
        )
    ]
    for load in loads:
        load.start()

    for n, source in ((0, qn), (1, gn)):
        loads[n].wait()
        for i in range(4):
            x = source[32 * i:32 * i + 32, :].astype(F32)
            qg[1, n, 16 * i:16 * i + 16, :] = jnp.concatenate([x[0:8], x[16:24]], 0).astype(BF16)
            qg[1, n, 64 + 16 * i:80 + 16 * i, :] = jnp.concatenate([x[8:16], x[24:32]], 0).astype(BF16)
    for n, source in ((0, ltn), (1, rdn)):
        loads[2 + n].wait()
        pieces = [source[:, r, TS * s:TS * s + TS] for s in (0, 1) for r in range(TS)]
        lro[1, 8 * n:8 * n + heads, :] = jnp.concatenate(pieces, 1)

    pl.semaphore_wait(barrier, 8 + (nx - 1) + (ny - 1) + (nl - 1) + (nz - 1) + 1)

    def qg_copy(n, c):
        dr, dc = STEPS[n]
        return pltpu.make_async_remote_copy(
            src_ref=qg.at[1, :, rows_of(-dc), lanes(c)],
            dst_ref=qg.at[block_of(dr, dc), :, rows_of(dc), lanes(c)],
            send_sem=qg_ss.at[c, n], recv_sem=qg_rs.at[c, n],
            device_id=at(-dr, -dc), device_id_type=MESH,
        )

    def forward_x(dr, t, c):
        return pltpu.make_async_remote_copy(
            src_ref=qg.at[block_of(dr, 0), :, rows_of(t), lanes(c)],
            dst_ref=qg.at[block_of(dr, -t), :, rows_of(-t), lanes(c)],
            send_sem=fw_ss.at[c, 2 * bit(dr) + bit(t)], recv_sem=qg_rs.at[c, STEPS.index((dr, -t))],
            device_id=at(0, t), device_id_type=MESH,
        )

    def forward_z(e, s, c):
        return pltpu.make_async_remote_copy(
            src_ref=qg.at[block_of(0, s), :, rows_of(s), lanes(c)],
            dst_ref=qg.at[block_of(-e, s), :, rows_of(s), lanes(c)],
            send_sem=fw_ss.at[c, 4 + 2 * bit(e) + bit(s)], recv_sem=qg_rs.at[c, STEPS.index((-e, s))],
            device_id=at(e, 0), device_id_type=MESH,
        )

    def hop_copy(dr):
        return pltpu.make_async_remote_copy(
            src_ref=qg.at[1, :, :, lanes(CHUNKS - 1)], dst_ref=held.at[bit(dr)],
            send_sem=hp_ss.at[bit(dr)], recv_sem=hp_rs.at[bit(dr)],
            device_id=(il * nz + lax.rem(iz - dr + nz, nz), iw, it), device_id_type=MESH,
        )

    def hop_forward(dr):
        return pltpu.make_async_remote_copy(
            src_ref=held.at[bit(dr)], dst_ref=qg.at[block_of(dr, 0), :, :, lanes(CHUNKS - 1)],
            send_sem=hf_ss.at[bit(dr)], recv_sem=qg_rs.at[CHUNKS - 1, STEPS.index((dr, 0))],
            device_id=(lax.rem(ia - dr * nz + nh, nh), iw, it), device_id_type=MESH,
        )

    def lr_copy(n):
        dr, dc = STEPS[n]
        return pltpu.make_async_remote_copy(
            src_ref=lro.at[1], dst_ref=lrx.at[n],
            send_sem=lr_ss.at[n], recv_sem=lr_rs.at[n],
            device_id=at(-dr, -dc), device_id_type=MESH,
        )

    def dq_copy(n, c):
        dr, dc = STEPS[n]
        return pltpu.make_async_remote_copy(
            src_ref=dq_send.at[block_of(dr, dc), rows_of(dc), lanes(c)],
            dst_ref=dq_recv.at[block_of(-dr, -dc), rows_of(-dc), lanes(c)],
            send_sem=dq_ss.at[c, n], recv_sem=dq_rs.at[c, n],
            device_id=at(dr, dc), device_id_type=MESH,
        )

    def corner_x(dr, s, c):
        return pltpu.make_async_remote_copy(
            src_ref=dq_send.at[block_of(dr, s), rows_of(s), lanes(c)],
            dst_ref=cx.at[bit(dr), bit(-s), :, lanes(c)],
            send_sem=co_ss.at[c, 2 * bit(dr) + bit(s)], recv_sem=cx_rs.at[c, 2 * bit(dr) + bit(-s)],
            device_id=at(0, s), device_id_type=MESH,
        )

    def corner_z(dr, s, c):
        return pltpu.make_async_remote_copy(
            src_ref=dq_send.at[block_of(dr, s), rows_of(s), lanes(c)],
            dst_ref=cz.at[bit(-dr), bit(s), :, lanes(c)],
            send_sem=co_ss.at[c, 2 * bit(dr) + bit(s)], recv_sem=cz_rs.at[c, 2 * bit(-dr) + bit(s)],
            device_id=at(dr, 0), device_id_type=MESH,
        )

    pairs = [(a, b) for a in SIDES for b in SIDES]
    has = {dr: there(dr) for dr in SIDES}
    mine_x = {(dr, s): both(has[dr], by_x((ia, iw), dr, s)) for dr, s in pairs}
    mine_z = {(dr, s): both(has[dr], by_z((ia, iw), dr, s)) for dr, s in pairs}
    mine_s = {(dr, s): both(has[dr], straight((ia, iw), dr, s)) for dr, s in pairs}
    relay_x = {(dr, t): both(has[dr], by_x(place(0, t), dr, -t)) for dr, t in pairs}
    relay_z = {(e, s): both(has[e], by_z(place(e, 0), -e, s)) for e, s in pairs}
    to_s = {(a, b): both(has[a], straight(place(a, b), -a, -b)) for a, b in pairs}
    at_seam = {s: seam(iw, s) for s in SIDES}
    crowded = {-1: ix == nx - 1, 1: ix == 0}
    hops = {
        -1: both(crowded[-1], both(iz == nz - 1, has[1])),
        1: both(crowded[1], both(iz == 0, has[-1])),
    }
    relays = {
        -1: both(crowded[-1], both(iz == 0, ia + nz < nh)),
        1: both(crowded[1], both(iz == nz - 1, ia >= nz)),
    }
    passes = {dr: both(has[-dr], jnp.logical_not(hops[dr])) for dr in SIDES}
    diagonal = [(a, b) for a, b in pairs if a != b]

    for n in range(8):
        lr_copy(n).start()
    for c in range(CHUNKS):
        for s in SIDES:
            qg_copy(STEPS.index((0, s)), c).start()
        for dr in SIDES:
            @pl.when(passes[dr] if c == CHUNKS - 1 else has[-dr])
            def _():
                qg_copy(STEPS.index((dr, 0)), c).start()

            if c == CHUNKS - 1:
                @pl.when(hops[dr])
                def _():
                    hop_copy(dr).start()
        for a, b in diagonal:
            @pl.when(to_s[a, b])
            def _():
                qg_copy(STEPS.index((-a, -b)), c).start()
    for dr in SIDES:
        @pl.when(jnp.logical_not(has[dr]))
        def _():
            qg[dr + 1] = jnp.zeros(qg.shape[1:], BF16)
            qg[dr + 4] = jnp.zeros(qg.shape[1:], BF16)
            dq_recv[dr + 1] = jnp.zeros(dq_recv.shape[1:], BF16)
    loads[5].wait()
    live = lax.broadcasted_iota(jnp.int32, (128, 128), 0) < plen_ref[0]
    for h in range(heads):
        hs = slice(HD * h, HD * h + HD)
        k, v, q, g = pkv[0, :, hs], pkv[1, :, hs], qg[1, 0, :, hs], qg[1, 1, :, hs]
        p = jnp.exp(jnp.where(live, nt(k, q) * factor - lro[1, h:h + 1, :], -BIG))
        ds = (factor * p * (nt(v, g) - lro[1, 8 + h:9 + h, :])).astype(BF16)
        dk = nn(ds, q).reshape(nw, tr, HD)
        dv = nn(p.astype(BF16), g).reshape(nw, tr, HD)
        ps[:, :, hs] = jnp.concatenate([dk, dv], 1).astype(BF16)
        dqf[1, :, hs] = tn(ds, k)

    def pa_copy(i):
        return pltpu.make_async_remote_copy(
            src_ref=ps.at[pl.ds(lax.rem(ix + i, nx) * ny, ny)], dst_ref=pa.at[ix],
            send_sem=pa_ss.at[i], recv_sem=pa_rs.at[i], device_id=(ia, x_peer(i), it), device_id_type=MESH,
        )

    def pb_copy(i):
        return pltpu.make_async_remote_copy(
            src_ref=s1.at[lax.rem(iy + i, ny)], dst_ref=pb.at[iy],
            send_sem=pb_ss.at[i], recv_sem=pb_rs.at[i], device_id=(ia, y_peer(i), it), device_id_type=MESH,
        )

    def p2_copy(i):
        return pltpu.make_async_remote_copy(
            src_ref=u1.at[il], dst_ref=u1.at[il], send_sem=p2_ss.at[i],
            recv_sem=p2_rs.at[i], device_id=(l_peer(i), iw, it), device_id_type=MESH,
        )

    def p3_copy(i):
        return pltpu.make_async_remote_copy(
            src_ref=vz.at[iz], dst_ref=vz.at[iz], send_sem=p3_ss.at[i],
            recv_sem=p3_rs.at[i], device_id=(z_peer(i), iw, it), device_id_type=MESH,
        )

    def cy_copy(i):
        own_slot = ix * ny + iy
        return pltpu.make_async_remote_copy(
            src_ref=c4.at[own_slot], dst_ref=c4.at[own_slot],
            send_sem=cy_ss.at[i], recv_sem=cy_rs.at[i], device_id=(ia, y_peer(i), it), device_id_type=MESH,
        )

    def cw_copy(i):
        slots = pl.ds(ix * ny, ny)
        return pltpu.make_async_remote_copy(
            src_ref=c4.at[slots], dst_ref=c4.at[slots],
            send_sem=cw_ss.at[i], recv_sem=cw_rs.at[i], device_id=(ia, x_peer(i), it), device_id_type=MESH,
        )

    c3_copy = pltpu.make_async_remote_copy(
        src_ref=c3.at[0], dst_ref=c3.at[1], send_sem=c3_ss, recv_sem=c3_rs,
        device_id=(ia, iw, 1 - it), device_id_type=MESH,
    )

    for i in range(1, nx):
        pa_copy(i).start()

    loads[4].wait()
    cols = 2 * nw
    table = nb.shape[1]
    tiles = [(r - 1, c) for r in range(3) for c in (0, 1)] + [(r - 1, c) for r in range(3) for c in (-1, 2)]
    which = lax.broadcasted_iota(jnp.int32, (16, table), 0)
    numbers = jnp.full((16, table), -5, jnp.int32)
    for n, (r, c) in enumerate(tiles):
        row, col = ia + r, 2 * iw + c
        fine = (row >= 0) & (row < nh) & (col >= 0) & (col < cols)
        numbers = jnp.where(which == n, jnp.where(fine, row * cols + col, -5), numbers)
    chosen = jnp.where(lax.broadcasted_iota(jnp.int32, (16, table), 1) == numbers, 1.0, 0.0)
    lane = lax.broadcasted_iota(jnp.int32, (1, 128), 1)
    for side in range(2):
        hit = jnp.max(jnp.where(nb[...] == ia * cols + 2 * iw + side, 1.0, 0.0), axis=0, keepdims=True)
        hit = jnp.broadcast_to(jnp.max(chosen * hit, axis=1, keepdims=True), (16, 128))
        for b in range(6):
            pen[b, side:side + 1, :] = BIG * (1.0 - jnp.where(lane < 64, hit[2 * b:2 * b + 1], hit[2 * b + 1:2 * b + 2]))

    loads[6].wait()

    def attend(b, c=None, first=False):
        for h in range(heads) if c is None else range(per_chunk * c, per_chunk * (c + 1)):
            hs = slice(HD * h, HD * h + HD)
            k, v, q, g = kv[0, :, hs], kv[1, :, hs], qg[b, 0, :, hs], qg[b, 1, :, hs]
            total = (lro[b, h:h + 1, :] + pen[b, 0:2, :]).reshape(1, 2, 1, 128)
            p = jnp.exp(nt(k, q).reshape(TS, 2, TS, 128) * factor - total).reshape(128, 128)
            ds = (factor * p * (nt(v, g) - lro[b, 8 + h:9 + h, :])).astype(BF16)
            dk, dv = nn(ds, q), nn(p.astype(BF16), g)
            if first:
                dkv_acc[0, :, hs] = dk
                dkv_acc[1, :, hs] = dv
                dqf[b, :, hs] += tn(ds, k)
            else:
                dkv_acc[0, :, hs] += dk
                dkv_acc[1, :, hs] += dv
                dqf[b, :, hs] = tn(ds, k)

    def totals_centre(n):
        lr_copy(n).wait_recv()
        lro[block_of(*STEPS[n])] = lrx[n]

    def totals_outer(west, east):
        lr_copy(west).wait_recv()
        lr_copy(east).wait_recv()
        both = jnp.where(lax.broadcasted_iota(jnp.int32, (16, 128), 1) < 64, lrx[east], lrx[west])
        lro[block_of(*STEPS[west])] = pltpu.roll(both, 64, 1)

    def beside_arrives(c):
        for s in SIDES:
            qg_copy(STEPS.index((0, s)), c).wait_recv()
            for e in SIDES:
                @pl.when(relay_z[e, s])
                def _():
                    forward_z(e, s, c).start()

    def above_below_arrive(c):
        for dr in SIDES:
            @pl.when(has[dr])
            def _():
                qg_copy(STEPS.index((dr, 0)), c).wait_recv()
            for t in SIDES:
                @pl.when(relay_x[dr, t])
                def _():
                    forward_x(dr, t, c).start()

    def send_beside(c, s):
        dq_send[4, rows_of(s), lanes(c)] = dqf[4, rows_of(s), lanes(c)].astype(BF16)
        dq_copy(STEPS.index((0, s)), c).start()

    def attend_beside(c):
        attend(4, c)
        for s in SIDES:
            @pl.when(jnp.logical_not(at_seam[s]))
            def _():
                send_beside(c, s)

    def attend_corners(c):
        for dr in SIDES:
            b = block_of(dr, 1)
            for s in SIDES:
                @pl.when(has[dr])
                def _():
                    qg_copy(STEPS.index((dr, s)), c).wait_recv()
            attend(b, c)
            dq_send[b, :, lanes(c)] = dqf[b, :, lanes(c)].astype(BF16)
            for s in SIDES:
                @pl.when(mine_x[dr, s])
                def _():
                    corner_x(dr, s, c).start()

                @pl.when(mine_z[dr, s])
                def _():
                    corner_z(dr, s, c).start()

                if (dr, s) in diagonal:
                    @pl.when(mine_s[dr, s])
                    def _():
                        dq_copy(STEPS.index((dr, s)), c).start()

    def fold(c):
        for s in SIDES:
            for e in SIDES:
                @pl.when(relay_z[e, s])
                def _():
                    corner_z(-e, s, c).wait_recv()
                    dqf[4, rows_of(s), lanes(c)] += cz[bit(e), bit(s), :, lanes(c)].astype(F32)

            @pl.when(at_seam[s])
            def _():
                send_beside(c, s)
        for dr in SIDES:
            for t in SIDES:
                @pl.when(relay_x[dr, t])
                def _():
                    corner_x(dr, -t, c).wait_recv()
                    dqf[dr + 1, rows_of(t), lanes(c)] += cx[bit(dr), bit(t), :, lanes(c)].astype(F32)
            dq_send[dr + 1, :, lanes(c)] = dqf[dr + 1, :, lanes(c)].astype(BF16)

            @pl.when(has[dr])
            def _():
                dq_copy(STEPS.index((dr, 0)), c).start()

    def sum_over_x():
        for i in range(1, nx):
            pa_copy(i).wait_recv()
        pa[ix] = ps[pl.ds(ix * ny, ny)]
        for j in range(ny):
            acc = pa[0, j].astype(F32)
            for i in range(1, nx):
                acc = acc + pa[i, j].astype(F32)
            s1[j] = acc
        for i in range(1, ny):
            pb_copy(i).start()

    def sum_over_y():
        for i in range(1, ny):
            pb_copy(i).wait_recv()
        pb[iy] = s1[iy]
        acc = pb[0]
        for j in range(1, ny):
            acc = acc + pb[j]
        u1[il] = acc
        for i in range(1, nl):
            p2_copy(i).start()

    def sum_over_rows():
        for i in range(1, nl):
            p2_copy(i).wait_recv()
        acc = u1[0]
        for j in range(1, nl):
            acc = acc + u1[j]
        vz[iz] = acc.astype(BF16)
        for i in range(1, nz):
            p3_copy(i).start()

    def project():
        for i in range(1, nz):
            p3_copy(i).wait_recv()
        loads[7].wait()
        acc = vz[0].astype(F32)
        for j in range(1, nz):
            acc = acc + vz[j].astype(F32)
        acc = acc.astype(BF16)
        c3[0] = nt(acc[:tr], proj[0]) + nt(acc[tr:], proj[1])
        c3_copy.start()

    def gather_over_y():
        c3_copy.wait_recv()
        c4[ix * ny + iy] = c3[0] + c3[1]
        for i in range(1, ny):
            cy_copy(i).start()

    def gather_over_x():
        for i in range(1, ny):
            cy_copy(i).wait_recv()
        for i in range(1, nx):
            cw_copy(i).start()

    def write_context():
        for i in range(1, nx):
            cw_copy(i).wait_recv()
        ctx_out[...] = c4[...].reshape(nw * tr, c4.shape[2]).T

    def write_keys():
        for n in range(2):
            for i in range(4):
                keys_low[n, 32 * i:32 * i + 32, :] = dkv_acc[n, 32 * i:32 * i + 32, :].astype(BF16)

    def write_queries():
        for c in range(CHUNKS):
            for s in SIDES:
                dq_copy(STEPS.index((0, s)), c).wait_recv()
            for dr in SIDES:
                @pl.when(has[-dr])
                def _():
                    dq_copy(STEPS.index((dr, 0)), c).wait_recv()
            for a, b in diagonal:
                @pl.when(to_s[a, b])
                def _():
                    dq_copy(STEPS.index((-a, -b)), c).wait_recv()
                    dqf[1, rows_of(b), lanes(c)] += dq_recv[block_of(a, b), rows_of(b), lanes(c)].astype(F32)
        for i in range(4):
            sums = []
            for start in (16 * i, 64 + 16 * i):
                rows = slice(start, start + 16)
                x = dqf[1, rows, :]
                for b in (0, 2, 4):
                    x = x + dq_recv[b, rows, :].astype(F32)
                sums.append(x)
            a, b = sums
            dq_out[32 * i:32 * i + 32, :] = jnp.concatenate([a[0:8], b[0:8], a[8:16], b[8:16]], 0).astype(BF16)

    attend(1, first=True)
    for dr in SIDES:
        @pl.when(relays[dr])
        def _():
            hop_copy(dr).wait_recv()
            hop_forward(dr).start()
    totals_outer(2, 3)
    beside_arrives(0)
    sum_over_x()
    for c in range(1, CHUNKS):
        beside_arrives(c)
    totals_centre(0)
    totals_centre(1)
    above_below_arrive(0)
    attend_beside(0)
    sum_over_y()
    for c in range(1, CHUNKS):
        above_below_arrive(c)
    for c in range(1, CHUNKS):
        attend_beside(c)
    attend(0, 0)
    attend(2, 0)
    sum_over_rows()
    for c in range(1, CHUNKS):
        attend(0, c)
        attend(2, c)
    totals_outer(4, 5)
    totals_outer(6, 7)
    attend_corners(0)
    project()
    for c in range(1, CHUNKS):
        attend_corners(c)
    gather_over_y()
    write_keys()
    key_move = pltpu.make_async_copy(keys_low, dkv_out, key_sem)
    key_move.start()
    for c in range(CHUNKS):
        fold(c)
    gather_over_x()
    write_queries()
    write_context()
    key_move.wait()

    for c in range(CHUNKS):
        for s in SIDES:
            qg_copy(STEPS.index((0, s)), c).wait_send()
            dq_copy(STEPS.index((0, s)), c).wait_send()

            @pl.when(passes[s] if c == CHUNKS - 1 else has[-s])
            def _():
                qg_copy(STEPS.index((s, 0)), c).wait_send()

            @pl.when(has[s])
            def _():
                dq_copy(STEPS.index((s, 0)), c).wait_send()
        for a, b in diagonal:
            @pl.when(to_s[a, b])
            def _():
                qg_copy(STEPS.index((-a, -b)), c).wait_send()

            @pl.when(mine_s[a, b])
            def _():
                dq_copy(STEPS.index((a, b)), c).wait_send()
        for a, b in pairs:
            @pl.when(both(has[a], jnp.logical_not(mine_s[a, b])))
            def _():
                corner_x(a, b, c).wait_send()

            @pl.when(relay_x[a, b])
            def _():
                forward_x(a, b, c).wait_send()

            @pl.when(relay_z[a, b])
            def _():
                forward_z(a, b, c).wait_send()
    for dr in SIDES:
        @pl.when(hops[dr])
        def _():
            hop_copy(dr).wait_send()

        @pl.when(relays[dr])
        def _():
            hop_forward(dr).wait_send()
    for n in range(8):
        lr_copy(n).wait_send()
    for i in range(1, nx):
        pa_copy(i).wait_send()
        cw_copy(i).wait_send()
    for i in range(1, ny):
        pb_copy(i).wait_send()
        cy_copy(i).wait_send()
    c3_copy.wait_send()
    for i in range(1, nl):
        p2_copy(i).wait_send()
    for i in range(1, nz):
        p3_copy(i).wait_send()


def deliver(a_in, b_in, c_in, a_out, b_out, c_out, a_mid, b_mid, c_mid, in_sem, out_sem):
    parts = [(b_in, b_mid, b_out), (a_in, a_mid, a_out), (c_in, c_mid, c_out)]
    reads = [pltpu.make_async_copy(src, mid, in_sem.at[n]) for n, (src, mid, _) in enumerate(parts)]
    writes = [pltpu.make_async_copy(mid, dst, out_sem.at[n]) for n, (_, mid, dst) in enumerate(parts)]
    for read in reads:
        read.start()
    for read, write in zip(reads, writes):
        read.wait()
        write.start()
    for write in writes:
        write.wait()


def solution(mesh):
    nh, nw = mesh.shape["ha"], mesh.shape["wa"]
    nx = min(RING_X, nw)
    ny = nw // nx
    nz = min(RING_Z, nh)
    nl = nh // nz

    def local(queries, keys_values, grad_out, log_totals, row_deltas, prompt_kv, prompt_proj, neighbours, prompt_length):
        rows_here, cols_here, width = queries.shape
        heads = log_totals.shape[-1]
        cells = rows_here * cols_here
        text = prompt_kv.shape[1]
        outs = prompt_proj.shape[1]
        tr = text // nw
        any_space = pl.BlockSpec(memory_space=pl.ANY)
        vmem = pl.BlockSpec(memory_space=pltpu.VMEM)
        dma = pltpu.SemaphoreType.DMA
        two = lambda n: [dma((n,)), dma((n,))]
        dq, dkv, ctx = pl.pallas_call(
            functools.partial(kernel, nh, nw, heads),
            out_shape=(
                jax.ShapeDtypeStruct((cells, width), BF16),
                jax.ShapeDtypeStruct((2, cells, width), BF16),
                jax.ShapeDtypeStruct((outs, text), F32),
            ),
            in_specs=[any_space] * 8 + [pl.BlockSpec(memory_space=pltpu.SMEM)],
            out_specs=(vmem, any_space, vmem),
            scratch_shapes=[
                pltpu.VMEM((2, cells, width), BF16),
                dma,
                pltpu.VMEM((cells, width), BF16),
                pltpu.VMEM((2, cells, width), BF16),
                pltpu.VMEM((cells, width), BF16),
                pltpu.VMEM((heads, rows_here, cols_here), F32),
                pltpu.VMEM((heads, rows_here, cols_here), F32),
                pltpu.VMEM((2, text, width), BF16),
                pltpu.VMEM((2, outs, width), BF16),
                pltpu.VMEM(neighbours.shape[::-1], jnp.int32),
                pltpu.VMEM((6, 2, cells, width), BF16),
                pltpu.VMEM((2, 2, cells, width // CHUNKS), BF16),
                pltpu.VMEM((8, 16, cells), F32),
                pltpu.VMEM((6, 16, cells), F32),
                pltpu.VMEM((6, 8, cells), F32),
                pltpu.VMEM((6, cells, width), F32),
                pltpu.VMEM((6, cells, width), BF16),
                pltpu.VMEM((6, cells, width), BF16),
                pltpu.VMEM((2, 2, CELLS, width), BF16),
                pltpu.VMEM((2, 2, CELLS, width), BF16),
                pltpu.VMEM((2, cells, width), F32),
                pltpu.VMEM((nw, 2 * tr, width), BF16),
                pltpu.VMEM((nx, ny, 2 * tr, width), BF16),
                pltpu.VMEM((ny, 2 * tr, width), F32),
                pltpu.VMEM((ny, 2 * tr, width), F32),
                pltpu.VMEM((nl, 2 * tr, width), F32),
                pltpu.VMEM((nz, 2 * tr, width), BF16),
                pltpu.VMEM((2, tr, outs), F32),
                pltpu.VMEM((nw, tr, outs), F32),
                dma((8,)),
                dma((CHUNKS, 8)), dma((CHUNKS, 8)), dma((CHUNKS, 8)), dma((2,)), *two(2), *two(8),
                dma((CHUNKS, 8)), dma((CHUNKS, 8)), dma((CHUNKS, 4)), dma((CHUNKS, 4)), dma((CHUNKS, 4)),
                *two(nx), *two(ny), *two(nl), *two(nz), dma, dma, *two(ny), *two(nx),
            ],
            compiler_params=pltpu.CompilerParams(
                collective_id=0, has_side_effects=True, vmem_limit_bytes=63 * 2**20
            ),
            name="tile_attention_grads",
        )(
            queries.reshape(cells, width), keys_values.reshape(2, cells, width), grad_out.reshape(cells, width),
            jnp.transpose(log_totals, (2, 0, 1)), jnp.transpose(row_deltas, (2, 0, 1)),
            prompt_kv, prompt_proj, neighbours.T, prompt_length,
        )
        results = (dq, dkv, ctx)
        dq, dkv, ctx = pl.pallas_call(
            deliver,
            out_shape=tuple(jax.ShapeDtypeStruct(x.shape, x.dtype) for x in results),
            in_specs=[any_space] * 3,
            out_specs=(any_space,) * 3,
            scratch_shapes=[pltpu.VMEM(x.shape, x.dtype) for x in results] + two(3),
            compiler_params=pltpu.CompilerParams(vmem_limit_bytes=62 * 2**20),
            name="deliver",
        )(*results)
        return (
            dq.reshape(rows_here, cols_here, width),
            dkv.reshape(2, rows_here, cols_here, width),
            ctx.T,
        )

    placed = P("ha", "wa", "ta")
    return jax.shard_map(
        local,
        mesh=mesh,
        in_specs=(placed, P(None, "ha", "wa", "ta"), placed, placed, placed, P(None, None, "ta"), P(None, "ha", "ta"), P(), P()),
        out_specs=(placed, P(None, "ha", "wa", "ta"), P(None, "ha")),
        check_vma=False,
    )
```
